128 devices in a mesh: attn: 8 (over x, core), ep: 16 (over y, z).
Axes of the slice: x: 4, y: 4, z: 4, core: 2. Of those that a mesh axis runs over, the one named last changes fastest.
Arguments:
- residual: bfloat16 [2, 128, 6144], P(None, ('attn', 'ep')), may hold values from -6 to 6
- query: bfloat16 [2, 128, 6144], P(None, ('attn', 'ep')), may hold values from -6 to 6
- new_key: bfloat16 [2, 128, 1024], P(None, ('attn', 'ep')), may hold values from -6 to 6
- new_value: bfloat16 [2, 128, 1024], P(None, ('attn', 'ep')), may hold values from -6 to 6
- key_cache: bfloat16 [2, 128, 512, 1024], P(None, ('attn', 'ep')), may hold values from -6 to 6
- value_cache: bfloat16 [2, 128, 512, 1024], P(None, ('attn', 'ep')), may hold values from -6 to 6
- lengths: int32 [2, 128], P(None, ('attn', 'ep')), may hold values from 2 to 512, as said below
- expert_ids: int32 [2, 128, 2], P(None, ('attn', 'ep')), may hold values from 0 to 7, all different within a row; in each aligned block of 16 rows (0 to 15, 16 to 31, ..., all dimensions but the last counted through in order) at most 6 rows name the same one
- norm_gain: float32 [6144], replicated, may hold values from 0.5 to 2
- router: bfloat16 [6144, 8], replicated, may hold values from -0.078125 to 0.078125
- w_gate: bfloat16 [16, 6144, 4096], P('ep', None, 'attn'), may hold values from -0.078125 to 0.078125
- w_up: bfloat16 [16, 6144, 4096], P('ep', None, 'attn'), may hold values from -0.078125 to 0.078125
- w_down: bfloat16 [16, 4096, 6144], P('ep', 'attn'), may hold values from -0.0625 to 0.0625
Outputs:
- mixed: bfloat16 [2, 128, 6144], P(None, ('attn', 'ep'))
The draws below stay inside these ranges and needn't reach their ends.
Inputs may be any that keep to these rules, and one draw needn't show every extreme that they name: `expert_ids`: the two ids of a row differ. In each micro-batch, each aligned block of 16 rows (the rows of one index of attn) names one expert at most 6 times, and some block reaches 6. `lengths`: in each micro-batch some row has all 512 positions valid.
All inputs are finite; a program needn't handle non-finite values.
Results may differ from the reference program's by a relative error of at most 0.019.
Values may be sent and summed in bfloat16 or wider, within the bound.
No kernel may reach another device: no remote copies, remote signals or barrier semaphores. Data moves between devices by JAX's collectives and lax.ppermute only.
A program may use at most 128 MiB of HBM per device.

```python
import math
import jax
import jax.numpy as jnp
import numpy as np
from jax import lax

D = 6144
KVH = 8
HD = 128
FFW = 8192
MB = 2
ROWS_DEV = 1
CTX = 512
EXPERTS = 8
CAP = 6
ROWS_MB = 128
N_ATTN = 8
N_EP = 16


def draw_query(key, part):
    key = jax.random.fold_in(key, 3)
    drawn = jax.random.truncated_normal(key, -6.0, 6.0, (MB, ROWS_MB, D), jnp.float32)
    return drawn.astype(jnp.bfloat16)


def draw_key_cache(key, part):
    key = jax.random.fold_in(key, 5)
    drawn = jax.random.truncated_normal(key, -6.0, 6.0, (MB, ROWS_MB, CTX, KVH * HD), jnp.float32)
    return drawn.astype(jnp.bfloat16)


def draw_lengths(key, part):
    key = jax.random.fold_in(key, 7)
    first_key, second_key = jax.random.split(key)
    values = jax.random.randint(first_key, (MB, ROWS_MB), 2, CTX + 1)
    longest = jax.random.randint(second_key, (MB,), 0, ROWS_MB)
    return values.at[jnp.arange(MB), longest].set(CTX).astype(jnp.int32)


def shard_levels(own_key, shape, cuts, low, top_value):
    factor_of = 1.0
    for dim, shards_of in cuts:
        steps = jax.random.uniform(jax.random.fold_in(jax.random.fold_in(own_key, 6), dim), (shards_of,), jnp.float32, low / len(cuts), top_value / len(cuts))
        factor_of = factor_of * jnp.repeat(jnp.exp(steps), shape[dim] // shards_of).reshape((-1,) + (1,) * (len(shape) - 1 - dim))
    return factor_of


def routed_block(rng, own, number, rows, number_of, top, most, skew):
    ranking = jax.random.permutation(rng, number_of)
    heavy_load, common = shares(number_of, rows * top, most, skew, True), shares(number_of, rows * top, most, skew, False)
    places = jnp.arange(number_of)

    def named(tallies, turn):
        used = int((tallies > 0).sum())
        fixed = max(1, used // 4)
        moved = fixed + (places - fixed + turn * (used - fixed)) % max(1, number_of - fixed)
        return jnp.zeros((number_of,), jnp.int32).at[ranking[jnp.where(places < fixed, places, moved)]].set(jnp.asarray(tallies, jnp.int32))

    tallies = jnp.where(number % 4 == 0, named(heavy_load, number // 4), named(common, number - number // 4 - 1))
    mixed = jax.random.permutation(jax.random.fold_in(own, 3), number_of)
    source_of, receiver = mixed[0:number_of // 2 * 2:2], mixed[1:number_of // 2 * 2:2]
    room = jnp.minimum(tallies[source_of] - 1, most - tallies[receiver]) // 2
    room = jnp.where((source_of == ranking[0]) | (receiver == ranking[0]) | (tallies[receiver] == 0), 0, jnp.maximum(room, 0))
    moved = jax.random.randint(jax.random.fold_in(own, 4), (number_of // 2,), 0, 1 << 20) % (room + 1)
    tallies = tallies.at[source_of].add(-moved).at[receiver].add(moved)
    labels = jnp.searchsorted(jnp.cumsum(tallies), jnp.arange(rows * top), side="right").astype(jnp.int32)
    grid = labels.reshape(top, rows).T
    grid = grid[jax.random.permutation(jax.random.fold_in(own, 1), rows)]
    turn = jax.random.randint(jax.random.fold_in(own, 2), (rows, 1), 0, top)
    return jnp.take_along_axis(grid, (jnp.arange(top)[None, :] + turn) % top, axis=1)


def shares(amount, total, limit, lean, full):
    portions = [(1 << 20) // math.isqrt(standing ** lean) + 1 for standing in range(1, amount + 1)]
    largest = limit if full else min(limit, max(-(-total // amount), total * portions[0] // sum(portions)))
    least = 1 if total - largest >= amount - 1 else 0
    holding, surplus = [largest] + [least] * (amount - 1), total - largest - least * (amount - 1)
    while surplus > 0:
        movable = [i for i in range(1, amount) if holding[i] < largest] or [i for i in range(1, amount) if holding[i] < limit]
        pool, remaining = sum([portions[i] for i in movable]), surplus
        for i in movable:
            more = min(limit - holding[i], max(1, remaining * portions[i] // pool), surplus)
            holding[i] = holding[i] + more
            surplus = surplus - more
    return np.array(holding)


def gaussian(rng, extent, spread, bound, pieces=(), kind=jnp.bfloat16):
    gain = shard_levels(rng, extent, pieces, -0.22, 0.18) if pieces else 1.0
    entries = jax.random.normal(rng, extent, jnp.float32) * spread * gain
    return jnp.minimum(jnp.maximum(entries, -bound), bound).astype(kind)


def setup_inputs(seed: int = 0) -> dict:
    arg_keys = jax.random.split(jax.random.key(seed), 14)
    residual = gaussian(arg_keys[0], (MB, ROWS_MB, D), 1.0, 6.0, ((1, 128),))
    query = draw_query(jax.random.fold_in(arg_keys[13], 71), 0)
    new_key = gaussian(arg_keys[2], (MB, ROWS_MB, KVH * HD), 1.0, 6.0, ((1, 128),))
    new_value = gaussian(arg_keys[3], (MB, ROWS_MB, KVH * HD), 1.0, 6.0, ((1, 128),))
    key_cache = draw_key_cache(jax.random.fold_in(arg_keys[13], 71), 0)
    value_cache = gaussian(arg_keys[5], (MB, ROWS_MB, CTX, KVH * HD), 1.0, 6.0, ((1, 128),))
    lengths = draw_lengths(jax.random.fold_in(arg_keys[13], 71), 0)
    expert_ids_keys = jax.random.split(jax.random.fold_in(arg_keys[7], 1), MB * ROWS_MB // (N_EP * ROWS_DEV))
    expert_ids_turns = jax.random.permutation(jax.random.fold_in(arg_keys[7], 3), MB * ROWS_MB // (N_EP * ROWS_DEV))
    expert_ids = jax.vmap(lambda own, number: routed_block(jax.random.fold_in(arg_keys[7], 2), own, number, N_EP * ROWS_DEV, EXPERTS, 2, CAP, 2))(expert_ids_keys, expert_ids_turns).reshape((MB, ROWS_MB, 2))
    norm_gain = jnp.clip(jnp.exp(jax.random.uniform(arg_keys[8], (D,), jnp.float32, math.log(0.5), math.log(2.0))), 0.5, 2.0)
    router = gaussian(arg_keys[9], (D, EXPERTS), D ** -0.5, 0.078125)
    w_gate = gaussian(arg_keys[10], (2 * EXPERTS, D, FFW // 2), D ** -0.5, 0.078125, ((0, 16), (2, 8)))
    w_up = gaussian(arg_keys[11], (2 * EXPERTS, D, FFW // 2), D ** -0.5, 0.078125, ((0, 16), (2, 8)))
    w_down = gaussian(arg_keys[12], (2 * EXPERTS, FFW // 2, D), FFW ** -0.5, 0.0625, ((0, 16), (1, 8)))
    return dict(residual=residual, query=query, new_key=new_key, new_value=new_value, key_cache=key_cache, value_cache=value_cache, lengths=lengths, expert_ids=expert_ids, norm_gain=norm_gain, router=router, w_gate=w_gate, w_up=w_up, w_down=w_down)


epsilon = 1e-05

def attend(query, new_key, new_value, key_cache, value_cache, lengths, kv_heads):
    row_total, features = query.shape
    context = key_cache.shape[1]
    head_size = new_key.shape[1] // kv_heads
    group_size = features // (kv_heads * head_size)
    score_scale = head_size ** (-0.5)
    queries = query.astype(jnp.float32).reshape(row_total, kv_heads, group_size, head_size)
    key_heads = key_cache.astype(jnp.float32).reshape(row_total, context, kv_heads, head_size)
    value_heads = value_cache.astype(jnp.float32).reshape(row_total, context, kv_heads, head_size)
    fresh_key = new_key.astype(jnp.float32).reshape(row_total, kv_heads, head_size)
    fresh_value = new_value.astype(jnp.float32).reshape(row_total, kv_heads, head_size)
    scores = jnp.einsum('rkgd,rtkd->rkgt', queries, key_heads) * score_scale
    own_score = jnp.einsum('rkgd,rkd->rkg', queries, fresh_key) * score_scale
    in_range = jnp.arange(context, dtype=jnp.int32)[None, :] < lengths[:, None]
    scores = jnp.where(in_range[:, None, None, :], scores, -jnp.inf)
    row_peak = jnp.maximum(lax.optimization_barrier(jnp.max(scores, axis=-1)), own_score)
    exp_terms = jnp.exp(scores - row_peak[..., None])
    own_exp = jnp.exp(own_score - row_peak)
    denominator = lax.optimization_barrier(jnp.sum(exp_terms, axis=-1)) + own_exp
    weights = (exp_terms / denominator[..., None]).astype(jnp.bfloat16)
    own_weight = (own_exp / denominator).astype(jnp.bfloat16)
    mixture = jnp.einsum('rkgt,rtkd->rkgd', weights.astype(jnp.float32), value_heads)
    mixture = mixture + own_weight.astype(jnp.float32)[..., None] * fresh_value[:, :, None, :]
    return mixture.reshape(row_total, features).astype(jnp.bfloat16)

def normalize(hidden, norm_gain):
    values = hidden.astype(jnp.float32)
    mean_square = lax.optimization_barrier(jnp.mean(values * values, axis=-1, keepdims=True))
    return (values * lax.rsqrt(mean_square + epsilon) * norm_gain.astype(jnp.float32)).astype(jnp.bfloat16)

def slot_table(ids, expert, capacity):
    leading = ids.shape[:-2]
    row_total = ids.shape[-2]
    flat_ids = ids.reshape(leading + (row_total * 2,))
    matches = (flat_ids == expert).astype(jnp.int32)
    position = (jnp.cumsum(matches, axis=-1) - matches).astype(jnp.int32)
    slot_ids = jnp.arange(capacity, dtype=jnp.int32)
    selected = (matches[..., None, :] == 1) & (position[..., None, :] == slot_ids[:, None])
    route_row = jnp.arange(row_total * 2, dtype=jnp.int32) // 2
    partner = flat_ids.reshape(leading + (row_total, 2))[..., ::-1].reshape(leading + (row_total * 2,))
    row_of = lax.optimization_barrier(jnp.sum(jnp.where(selected, route_row, 0), axis=-1)).astype(jnp.int32)
    other_of = (lax.optimization_barrier(jnp.sum(jnp.where(selected, partner[..., None, :] + 1, 0), axis=-1)) - 1).astype(jnp.int32)
    return (row_of, other_of)

def route_gate(rows, router, expert, other):
    logits = jnp.dot(rows, router, preferred_element_type=jnp.float32)
    columns = jnp.arange(router.shape[1], dtype=jnp.int32)[None, :]
    own_logit = lax.optimization_barrier(jnp.sum(jnp.where(columns == expert, logits, 0.0), axis=1))
    other_logit = lax.optimization_barrier(jnp.sum(jnp.where(columns == other[:, None], logits, 0.0), axis=1))
    larger = jnp.maximum(own_logit, other_logit)
    own_exp = jnp.exp(own_logit - larger)
    other_exp = jnp.exp(other_logit - larger)
    return jnp.where(other >= 0, own_exp / (own_exp + other_exp), 0.0)

def reference(residual, query, new_key, new_value, key_cache, value_cache, lengths, expert_ids, norm_gain, router, w_gate, w_up, w_down):
    attended = lax.map(lambda packed: attend(*packed, KVH), (query, new_key, new_value, key_cache, value_cache, lengths))
    stream = (residual.astype(jnp.float32) + attended.astype(jnp.float32)).astype(jnp.bfloat16)
    normed = normalize(stream, norm_gain)
    flat_normed = normed.reshape(MB * ROWS_MB, D)
    per_group = N_EP * ROWS_DEV
    grouped = expert_ids.reshape(MB, N_ATTN, per_group, 2)
    offsets = jnp.arange(N_ATTN, dtype=jnp.int32)[:, None] * per_group
    batch_offsets = jnp.arange(MB, dtype=jnp.int32)[:, None] * ROWS_MB

    def per_expert(carry, expert):
        row_of, other_of = slot_table(grouped, expert, CAP)
        global_row = (row_of + offsets).reshape(MB, N_ATTN * CAP) + batch_offsets
        positions = global_row.reshape(-1)
        rows = flat_normed[positions]
        gates = route_gate(rows, router, expert, other_of.reshape(-1))
        gate_full = jnp.concatenate([w_gate[2 * expert], w_gate[2 * expert + 1]], axis=1)
        up_full = jnp.concatenate([w_up[2 * expert], w_up[2 * expert + 1]], axis=1)
        down_full = jnp.concatenate([w_down[2 * expert], w_down[2 * expert + 1]], axis=0)
        gate_proj = jnp.dot(rows, gate_full, preferred_element_type=jnp.float32)
        up_proj = jnp.dot(rows, up_full, preferred_element_type=jnp.float32)
        activation = (jax.nn.silu(gate_proj) * up_proj).astype(jnp.bfloat16)
        outputs = jnp.dot(activation, down_full, preferred_element_type=jnp.float32) * gates[:, None]
        return (carry + jax.ops.segment_sum(outputs, positions, num_segments=MB * ROWS_MB), None)
    start_sum = jnp.zeros((MB * ROWS_MB, D), jnp.float32)
    expert_sum, unused = lax.scan(per_expert, start_sum, jnp.arange(EXPERTS, dtype=jnp.int32))
    mixed = stream.astype(jnp.float32) + expert_sum.reshape(MB, ROWS_MB, D)
    return mixed.astype(jnp.bfloat16)
```

```python
import functools

import jax
import jax.numpy as jnp
from jax import lax
from jax.experimental import pallas as pl
from jax.experimental.pallas import tpu as pltpu
from jax.sharding import Mesh, PartitionSpec as P

KV_HEADS = 8
HEAD = 128
CAP = 6
CORES = 2
LANES = 128
PARTS = 4
EPSILON = 1e-05

VMEM = pl.BlockSpec(memory_space=pltpu.VMEM)
SMEM = pl.BlockSpec(memory_space=pltpu.SMEM)
ANY = pl.BlockSpec(memory_space=pl.ANY)


def iota(shape, dim):
    return lax.broadcasted_iota(jnp.int32, shape, dim)


def attention_kernel(
    lengths, ids, query, residual, new_key, new_value, keys, values, gain, router,
    send, stream_out, gates_out,
    key_buf, value_buf, spread, rows, packed, sems,
):
    batches, features = query.shape
    context = keys.shape[1]
    heads = features // HEAD
    group = heads // KV_HEADS
    peers = send.shape[0] // CORES
    half = features // CORES
    piece = half // PARTS
    copies = []
    for row in range(batches):
        copies.append(
            (
                pltpu.make_async_copy(keys.at[row], key_buf.at[row], sems.at[2 * row]),
                pltpu.make_async_copy(values.at[row], value_buf.at[row], sems.at[2 * row + 1]),
            )
        )
    for pair in copies:
        for copy in pair:
            copy.start()
    rows[...] = jnp.zeros_like(rows)
    query_wide = query[...].astype(jnp.float32)
    key_wide = new_key[...].astype(jnp.float32)
    value_wide = new_value[...].astype(jnp.float32)
    spread[...] = jnp.zeros_like(spread)
    for row in range(batches):
        for head in range(heads):
            block, place = head // group, head % group
            spread[row, pl.ds(8 * block + place, 1), pl.ds(HEAD * block, HEAD)] = query_wide[
                row : row + 1, HEAD * head : HEAD * (head + 1)
            ]
    for row in range(batches):
        queries = spread[row]
        own = jnp.sum(queries * key_wide[row : row + 1], axis=1, keepdims=True) * HEAD**-0.5
        copies[row][0].wait()
        scores = (
            lax.dot_general(
                queries.astype(jnp.bfloat16),
                key_buf[row],
                (((1,), (1,)), ((), ())),
                preferred_element_type=jnp.float32,
            )
            * HEAD**-0.5
        )
        scores = jnp.where(iota(scores.shape, 1) < lengths[row], scores, -jnp.inf)
        peak = jnp.maximum(jnp.max(scores, axis=1, keepdims=True), own)
        terms = jnp.exp(scores - peak)
        own_term = jnp.exp(own - peak)
        total = jnp.sum(terms, axis=1, keepdims=True) + own_term
        weights = (terms / total).astype(jnp.bfloat16)
        own_weight = (own_term / total).astype(jnp.bfloat16).astype(jnp.float32)
        copies[row][1].wait()
        mixture = jnp.dot(weights, value_buf[row], preferred_element_type=jnp.float32)
        mixture = mixture + own_weight * value_wide[row : row + 1]
        for head in range(heads):
            block, place = head // group, head % group
            rows[row : row + 1, HEAD * head : HEAD * (head + 1)] = mixture[
                8 * block + place : 8 * block + place + 1, HEAD * block : HEAD * (block + 1)
            ]
    attended = rows[0:batches].astype(jnp.bfloat16).astype(jnp.float32)
    stream = (residual[...].astype(jnp.float32) + attended).astype(jnp.bfloat16)
    stream = stream.astype(jnp.float32)
    mean_square = jnp.sum(stream * stream, axis=1, keepdims=True) * (1.0 / features)
    normed = (stream * lax.rsqrt(mean_square + EPSILON) * gain[...]).astype(jnp.bfloat16)
    normed = normed.astype(jnp.float32)
    rows[0:batches] = normed
    logits = lax.dot_general(
        rows[...].astype(jnp.bfloat16),
        router[...],
        (((1,), (1,)), ((), ())),
        preferred_element_type=jnp.float32,
    )
    for core in range(CORES):
        for row in range(batches):
            for part in range(PARTS):
                start = core * half + part * piece
                place = row * PARTS + part
                packed[0, pl.ds(place, 1), 0:piece] = normed[row : row + 1, start : start + piece]
                packed[1, pl.ds(place, 1), 0:piece] = stream[row : row + 1, start : start + piece]
            lane = iota((PARTS, LANES), 1)
            names = jnp.where(lane == 0, ids[row, 0], jnp.where(lane == 1, ids[row, 1], 0))
            packed[0, pl.ds(row * PARTS, PARTS), piece : piece + LANES] = names.astype(jnp.float32)
        chunk = packed[0].astype(jnp.bfloat16)
        for peer in range(peers):
            send[core * peers + peer] = chunk
        stream_out[core] = packed[1, :, 0:piece].astype(jnp.bfloat16)
    for row in range(batches):
        lane = iota((1, logits.shape[1]), 1)
        own = logits[row : row + 1]
        first = jnp.sum(jnp.where(lane == ids[row, 0], own, 0.0), axis=1, keepdims=True)
        second = jnp.sum(jnp.where(lane == ids[row, 1], own, 0.0), axis=1, keepdims=True)
        larger = jnp.maximum(first, second)
        first, second = jnp.exp(first - larger), jnp.exp(second - larger)
        total = first + second
        expert = iota((PARTS, LANES), 1) // 2
        gates_out[pl.ds(row * PARTS, PARTS), :] = jnp.where(
            expert == ids[row, 0],
            first / total,
            jnp.where(expert == ids[row, 1], second / total, 0.0),
        )


def select_kernel(expert, received, chosen_out, places_out):
    count, width = received.shape
    piece = width - LANES
    slots = CORES * 2 * CAP
    here = expert[0].astype(jnp.float32)
    names = received[:, piece:].astype(jnp.float32)
    lane = iota(names.shape, 1)
    match = jnp.where((names == here) & (lane < 2), 1.0, 0.0)
    match = jnp.sum(match, axis=1, keepdims=True)
    a, b = iota((count, count), 0), iota((count, count), 1)
    span = 8 * (count // (8 * CORES))
    earlier = (a // span == b // span) & (a % 8 == b % 8) & (b < a)
    rank = jnp.dot(
        jnp.where(earlier, 1.0, 0.0).astype(jnp.bfloat16),
        jnp.broadcast_to(match, (count, LANES)).astype(jnp.bfloat16),
        preferred_element_type=jnp.float32,
    )
    r, col = iota((count, LANES), 0), iota((count, LANES), 1)
    part, batch, core = r % PARTS, (r % 8) // PARTS, r // span
    target = part * slots + core * (2 * CAP) + batch * CAP + rank.astype(jnp.int32)
    places = jnp.where((col == target) & (match > 0.5), 1.0, 0.0).astype(jnp.bfloat16)
    places_out[...] = places
    chosen = lax.dot_general(
        places,
        received[:, 0:piece],
        (((0,), (0,)), ((), ())),
        preferred_element_type=jnp.float32,
    ).astype(jnp.bfloat16).astype(jnp.float32)
    for part in range(PARTS):
        chosen_out[:, part * piece : (part + 1) * piece] = chosen[
            part * slots : (part + 1) * slots
        ].astype(jnp.bfloat16)


def expert_kernel(
    core, mine, other, w_gate, w_up, w_down, mine_out, other_out,
    gate_buf, up_buf, down_buf, sems,
):
    features, hidden = w_gate.shape
    half = features // CORES
    steps = 4
    width = half // steps
    c = core[0]
    up_copies, down_copies = [], []
    for h in range(CORES):
        base = jnp.where(c == h, 0, half)
        for s in range(steps):
            at = pl.ds(pl.multiple_of(base + s * width, width), width)
            index = 2 * (h * steps + s)
            pair = (
                pltpu.make_async_copy(w_gate.at[at], gate_buf.at[h, s], sems.at[index]),
                pltpu.make_async_copy(w_up.at[at], up_buf.at[h, s], sems.at[index + 1]),
            )
            for copy in pair:
                copy.start()
            up_copies.append(pair)
    for h in range(CORES):
        base = jnp.where(c == h, half, 0)
        for s in range(steps):
            at = pl.ds(pl.multiple_of(base + s * width, width), width)
            copy = pltpu.make_async_copy(
                w_down.at[:, at], down_buf.at[h, s], sems.at[4 * steps + h * steps + s]
            )
            copy.start()
            down_copies.append(copy)
    gate = jnp.zeros((mine.shape[0], hidden), jnp.float32)
    up = jnp.zeros((mine.shape[0], hidden), jnp.float32)
    for h, rows in enumerate((mine, other)):
        for s in range(steps):
            x = rows[:, s * width : (s + 1) * width]
            for copy in up_copies[h * steps + s]:
                copy.wait()
            gate += jnp.dot(x, gate_buf[h, s], preferred_element_type=jnp.float32)
            up += jnp.dot(x, up_buf[h, s], preferred_element_type=jnp.float32)
    act = (gate * (1.0 / (1.0 + jnp.exp(-gate))) * up).astype(jnp.bfloat16)
    for h, out in enumerate((other_out, mine_out)):
        for s in range(steps):
            down_copies[h * steps + s].wait()
            out[:, s * width : (s + 1) * width] = jnp.dot(
                act, down_buf[h, s], preferred_element_type=jnp.float32
            ).astype(jnp.bfloat16)


def spread_kernel(places, own, first, second, third, send):
    slots, width = own.shape
    piece = width // PARTS
    total = own[...].astype(jnp.float32) + first[...].astype(jnp.float32)
    total = total + second[...].astype(jnp.float32) + third[...].astype(jnp.float32)
    stacked = jnp.concatenate(
        [total[:, part * piece : (part + 1) * piece] for part in range(PARTS)]
        + [jnp.zeros((LANES - PARTS * slots, piece), jnp.float32)],
        axis=0,
    ).astype(jnp.bfloat16)
    send[...] = jnp.dot(places[...], stacked, preferred_element_type=jnp.float32).astype(
        jnp.bfloat16
    )


def combine_kernel(received, stream, gates, out, rows):
    peers = received.shape[0] // CORES
    piece = received.shape[2]
    half = piece * PARTS
    batches = out.shape[0]
    gate = gates[...]
    for core in range(CORES):
        total = jnp.zeros(received.shape[1:], jnp.float32)
        for peer in range(peers):
            total += received[core * peers + peer].astype(jnp.float32) * gate[:, peer : peer + 1]
        total += stream[core].astype(jnp.float32)
        for row in range(batches):
            for part in range(PARTS):
                start = core * half + part * piece
                place = row * PARTS + part
                rows[row : row + 1, start : start + piece] = total[place : place + 1]
    out[...] = rows[0:batches].astype(jnp.bfloat16)


def shards(
    residual, query, new_key, new_value, key_cache, value_cache, lengths, expert_ids,
    norm_gain, router, w_gate, w_up, w_down,
):
    batches, _, features = residual.shape
    context = key_cache.shape[2]
    kv_width = key_cache.shape[3]
    xs = lax.axis_size("x")
    peers = lax.axis_size("ep")
    half = features // CORES
    piece = half // PARTS
    slots = CORES * batches * CAP
    expert = lax.axis_index("ep") // 2
    core = lax.axis_index("core")
    f32, bf16 = jnp.float32, jnp.bfloat16
    big = pltpu.CompilerParams(vmem_limit_bytes=48 * 2**20)

    with jax.named_scope("attention"):
        send, stream, gates = pl.pallas_call(
            attention_kernel,
            out_shape=(
                jax.ShapeDtypeStruct((CORES * peers, 8, piece + LANES), bf16),
                jax.ShapeDtypeStruct((CORES, 8, piece), bf16),
                jax.ShapeDtypeStruct((8, LANES), f32),
            ),
            in_specs=[SMEM, SMEM, VMEM, VMEM, VMEM, VMEM, ANY, ANY, VMEM, VMEM],
            out_specs=(VMEM, VMEM, VMEM),
            scratch_shapes=[
                pltpu.VMEM((batches, context, kv_width), bf16),
                pltpu.VMEM((batches, context, kv_width), bf16),
                pltpu.VMEM((batches, 8 * KV_HEADS, kv_width), f32),
                pltpu.VMEM((8, features), f32),
                pltpu.VMEM((2, 8, piece + LANES), f32),
                pltpu.SemaphoreType.DMA((2 * batches,)),
            ],
            compiler_params=big,
            name="attention",
        )(
            lengths.reshape(batches),
            expert_ids.reshape(batches, 2),
            query.reshape(batches, features),
            residual.reshape(batches, features),
            new_key.reshape(batches, kv_width),
            new_value.reshape(batches, kv_width),
            key_cache.reshape(batches, context, kv_width),
            value_cache.reshape(batches, context, kv_width),
            norm_gain.reshape(1, features),
            router.T,
        )
    with jax.named_scope("rows_to_experts"):
        received = lax.all_to_all(send, ("core", "ep"), 0, 0, tiled=True)
    with jax.named_scope("select"):
        chosen, places = pl.pallas_call(
            select_kernel,
            out_shape=(
                jax.ShapeDtypeStruct((slots, half), bf16),
                jax.ShapeDtypeStruct((CORES * peers * 8, LANES), bf16),
            ),
            in_specs=[SMEM, VMEM],
            out_specs=(VMEM, VMEM),
            compiler_params=big,
            name="select",
        )(expert.reshape(1), received.reshape(CORES * peers * 8, piece + LANES))

    def along(array, step):
        return lax.ppermute(array, "x", [(i, (i + step) % xs) for i in range(xs)])

    def swap(array):
        return lax.ppermute(array, "core", [(0, 1), (1, 0)])

    with jax.named_scope("rows_along_x"):
        parts = [chosen] + [along(chosen, step) for step in range(1, xs)]
        mine = jnp.concatenate(parts, axis=0)
    with jax.named_scope("rows_between_cores"):
        other = swap(mine)
    with jax.named_scope("experts"):
        mine_sum, other_sum = pl.pallas_call(
            expert_kernel,
            out_shape=(jax.ShapeDtypeStruct(mine.shape, bf16),) * 2,
            in_specs=[SMEM, VMEM, VMEM, ANY, ANY, ANY],
            out_specs=(VMEM, VMEM),
            scratch_shapes=[
                pltpu.VMEM((2, 4, half // 4, w_gate.shape[2]), bf16),
                pltpu.VMEM((2, 4, half // 4, w_gate.shape[2]), bf16),
                pltpu.VMEM((2, 4, w_down.shape[1], half // 4), bf16),
                pltpu.SemaphoreType.DMA((24,)),
            ],
            compiler_params=big,
            name="experts",
        )(core.reshape(1), mine, other, w_gate[0], w_up[0], w_down[0])
    with jax.named_scope("sums_between_cores"):
        arrived = swap(other_sum)
        total = (mine_sum.astype(f32) + arrived.astype(f32)).astype(bf16)
    with jax.named_scope("sums_along_x"):
        total = total.reshape(xs, slots, half)
        backs = [along(total[step], xs - step) for step in range(1, xs)]
    with jax.named_scope("spread"):
        send = pl.pallas_call(
            spread_kernel,
            out_shape=jax.ShapeDtypeStruct((CORES * peers * 8, piece), bf16),
            in_specs=[VMEM] * (2 + len(backs)),
            out_specs=VMEM,
            compiler_params=big,
            name="spread",
        )(places, total[0], *backs)
    with jax.named_scope("sums_to_rows"):
        received = lax.all_to_all(
            send.reshape(CORES * peers, 8, piece), ("core", "ep"), 0, 0, tiled=True
        )
    with jax.named_scope("combine"):
        out = pl.pallas_call(
            combine_kernel,
            out_shape=jax.ShapeDtypeStruct((batches, features), bf16),
            in_specs=[VMEM, VMEM, VMEM],
            out_specs=VMEM,
            scratch_shapes=[pltpu.VMEM((8, features), f32)],
            compiler_params=big,
            name="combine",
        )(received, stream, gates)
    return out.reshape(batches, 1, features)


def solution(mesh):
    attn, ep = mesh.shape["attn"], mesh.shape["ep"]
    fine = Mesh(mesh.devices.reshape(attn // CORES, CORES, ep), ("x", "core", "ep"))
    rows = ("x", "core", "ep")
    in_specs = (
        P(None, rows, None),
        P(None, rows, None),
        P(None, rows, None),
        P(None, rows, None),
        P(None, rows, None, None),
        P(None, rows, None, None),
        P(None, rows),
        P(None, rows, None),
        P(),
        P(),
        P("ep", None, ("x", "core")),
        P("ep", None, ("x", "core")),
        P("ep", ("x", "core"), None),
    )
    return jax.shard_map(
        shards, mesh=fine, in_specs=in_specs, out_specs=P(None, rows, None), check_vma=False
    )
```

```python
import functools

import jax
import jax.numpy as jnp
from jax import lax
from jax.experimental import pallas as pl
from jax.experimental.pallas import tpu as pltpu
from jax.sharding import Mesh, PartitionSpec as P

KV_HEADS = 8
HEAD = 128
CAP = 6
CORES = 2
LANES = 128
PARTS = 4
EPSILON = 1e-05

VMEM = pl.BlockSpec(memory_space=pltpu.VMEM)
SMEM = pl.BlockSpec(memory_space=pltpu.SMEM)
ANY = pl.BlockSpec(memory_space=pl.ANY)


def iota(shape, dim):
    return lax.broadcasted_iota(jnp.int32, shape, dim)


def attention_kernel(
    expert, core, lengths_at, ids_at, query_at, residual_at, new_key_at, new_value_at, keys, values, gain_at,
    router_at, send, stream_out, gates_out,
    lengths, ids, query, residual, new_key, new_value, gain, router,
    key_buf, value_buf, spread, rows, packed, sems, small_sems,
):
    batches, features = query.shape
    heads = features // HEAD
    group = heads // KV_HEADS
    peers = send.shape[0] // CORES
    half = features // CORES
    piece = half // PARTS
    copies = []
    for row in range(batches):
        copies.append(
            (
                pltpu.make_async_copy(keys.at[row], key_buf.at[row], sems.at[2 * row]),
                pltpu.make_async_copy(values.at[row], value_buf.at[row], sems.at[2 * row + 1]),
            )
        )
    small = [
        pltpu.make_async_copy(source, target, small_sems.at[index])
        for index, (source, target) in enumerate(
            (
                (query_at, query),
                (new_key_at, new_key),
                (new_value_at, new_value),
                (residual_at, residual),
                (gain_at, gain),
                (router_at, router),
                (lengths_at, lengths),
                (ids_at, ids),
            )
        )
    ]
    for copy in small[:3]:
        copy.start()
    for copy in copies[0]:
        copy.start()
    for copy in small[3:]:
        copy.start()
    for pair in copies[1:]:
        for copy in pair:
            copy.start()
    rows[...] = jnp.zeros_like(rows)
    spread[...] = jnp.zeros_like(spread)
    for copy in small:
        copy.wait()
    query_wide = query[...].astype(jnp.float32)
    key_wide = new_key[...].astype(jnp.float32)
    value_wide = new_value[...].astype(jnp.float32)
    for row in range(batches):
        for head in range(heads):
            block, place = head // group, head % group
            spread[row, pl.ds(8 * block + place, 1), pl.ds(HEAD * block, HEAD)] = query_wide[
                row : row + 1, HEAD * head : HEAD * (head + 1)
            ]
    for row in range(batches):
        queries = spread[row]
        own = jnp.sum(queries * key_wide[row : row + 1], axis=1, keepdims=True) * HEAD**-0.5
        copies[row][0].wait()
        scores = (
            lax.dot_general(
                queries.astype(jnp.bfloat16),
                key_buf[row],
                (((1,), (1,)), ((), ())),
                preferred_element_type=jnp.float32,
            )
            * HEAD**-0.5
        )
        scores = jnp.where(iota(scores.shape, 1) < lengths[row], scores, -jnp.inf)
        peak = jnp.maximum(jnp.max(scores, axis=1, keepdims=True), own)
        terms = jnp.exp(scores - peak)
        own_term = jnp.exp(own - peak)
        total = jnp.sum(terms, axis=1, keepdims=True) + own_term
        weights = (terms / total).astype(jnp.bfloat16)
        own_weight = (own_term / total).astype(jnp.bfloat16).astype(jnp.float32)
        copies[row][1].wait()
        mixture = jnp.dot(weights, value_buf[row], preferred_element_type=jnp.float32)
        mixture = mixture + own_weight * value_wide[row : row + 1]
        for head in range(heads):
            block, place = head // group, head % group
            rows[row : row + 1, HEAD * head : HEAD * (head + 1)] = mixture[
                8 * block + place : 8 * block + place + 1, HEAD * block : HEAD * (block + 1)
            ]
    attended = rows[0:batches].astype(jnp.bfloat16).astype(jnp.float32)
    stream = (residual[...].astype(jnp.float32) + attended).astype(jnp.bfloat16)
    stream = stream.astype(jnp.float32)
    mean_square = jnp.sum(stream * stream, axis=1, keepdims=True) * (1.0 / features)
    normed = (stream * lax.rsqrt(mean_square + EPSILON) * gain[...]).astype(jnp.bfloat16)
    normed = normed.astype(jnp.float32)
    rows[0:batches] = normed
    logits = lax.dot_general(
        rows[...].astype(jnp.bfloat16),
        router[...],
        (((1,), (1,)), ((), ())),
        preferred_element_type=jnp.float32,
    )
    for side in range(CORES):
        for row in range(batches):
            for part in range(PARTS):
                start = side * half + part * piece
                place = row * PARTS + part
                packed[0, pl.ds(place, 1), 0:piece] = normed[row : row + 1, start : start + piece]
                packed[1, pl.ds(place, 1), 0:piece] = stream[row : row + 1, start : start + piece]
            lane = iota((PARTS, LANES), 1)
            names = jnp.where(lane == 0, ids[row, 0], jnp.where(lane == 1, ids[row, 1], 0))
            packed[0, pl.ds(row * PARTS, PARTS), piece : piece + LANES] = names.astype(jnp.float32)
        chunk = packed[0].astype(jnp.bfloat16)
        for peer in range(peers):
            send[side * peers + peer] = chunk
        stream_out[side] = packed[1, :, 0:piece].astype(jnp.bfloat16)
    for row in range(batches):
        lane = iota((1, logits.shape[1]), 1)
        own = logits[row : row + 1]
        first = jnp.sum(jnp.where(lane == ids[row, 0], own, 0.0), axis=1, keepdims=True)
        second = jnp.sum(jnp.where(lane == ids[row, 1], own, 0.0), axis=1, keepdims=True)
        larger = jnp.maximum(first, second)
        first, second = jnp.exp(first - larger), jnp.exp(second - larger)
        total = first + second
        expert = iota((PARTS, LANES), 1) // 2
        gates_out[pl.ds(row * PARTS, PARTS), :] = jnp.where(
            expert == ids[row, 0],
            first / total,
            jnp.where(expert == ids[row, 1], second / total, 0.0),
        )


def select_kernel(expert, received, chosen_out, places_out):
    count, width = received.shape
    piece = width - LANES
    slots = CORES * 2 * CAP
    here = expert[0].astype(jnp.float32)
    names = received[:, piece:].astype(jnp.float32)
    lane = iota(names.shape, 1)
    match = jnp.where((names == here) & (lane < 2), 1.0, 0.0)
    match = jnp.sum(match, axis=1, keepdims=True)
    a, b = iota((count, count), 0), iota((count, count), 1)
    span = 8 * (count // (8 * CORES))
    earlier = (a // span == b // span) & (a % 8 == b % 8) & (b < a)
    rank = jnp.dot(
        jnp.where(earlier, 1.0, 0.0).astype(jnp.bfloat16),
        jnp.broadcast_to(match, (count, LANES)).astype(jnp.bfloat16),
        preferred_element_type=jnp.float32,
    )
    r, col = iota((count, LANES), 0), iota((count, LANES), 1)
    part, batch, core = r % PARTS, (r % 8) // PARTS, r // span
    target = part * slots + core * (2 * CAP) + batch * CAP + rank.astype(jnp.int32)
    places = jnp.where((col == target) & (match > 0.5), 1.0, 0.0).astype(jnp.bfloat16)
    places_out[...] = places
    chosen = lax.dot_general(
        places,
        received[:, 0:piece],
        (((0,), (0,)), ((), ())),
        preferred_element_type=jnp.float32,
    ).astype(jnp.bfloat16).astype(jnp.float32)
    for part in range(PARTS):
        chosen_out[:, part * piece : (part + 1) * piece] = chosen[
            part * slots : (part + 1) * slots
        ].astype(jnp.bfloat16)


def fetch_kernel(after, gate_at, up_at, down_at, gate, up, down, ready, sems):
    pieces = 4
    copies = []
    for source, target in ((gate_at, gate), (up_at, up), (down_at, down)):
        rows = source.shape[0] // pieces
        for piece in range(pieces):
            at = pl.ds(piece * rows, rows)
            copies.append(
                pltpu.make_async_copy(source.at[at], target.at[at], sems.at[len(copies)])
            )
    for copy in copies:
        copy.start()
    ready[...] = jnp.zeros_like(ready)
    for copy in copies:
        copy.wait()


def join_kernel(ready, *refs):
    parts, out = refs[:-1], refs[-1]
    count = parts[0].shape[0]
    for index, part in enumerate(parts):
        out[index * count : (index + 1) * count, :] = part[...]


def near_kernel(core, rows, w_gate, w_up, gate_out, up_out):
    half = rows.shape[1]
    at = pl.ds(pl.multiple_of(core[0] * half, half), half)
    gate_out[...] = jnp.dot(rows[...], w_gate[at], preferred_element_type=jnp.float32)
    up_out[...] = jnp.dot(rows[...], w_up[at], preferred_element_type=jnp.float32)


def far_kernel(core, rows, gate, up, w_gate, w_up, w_down, act_out, out):
    half = rows.shape[1]
    at = pl.ds(pl.multiple_of((1 - core[0]) * half, half), half)
    total = gate[...] + jnp.dot(rows[...], w_gate[at], preferred_element_type=jnp.float32)
    other = up[...] + jnp.dot(rows[...], w_up[at], preferred_element_type=jnp.float32)
    act = (total * (1.0 / (1.0 + jnp.exp(-total))) * other).astype(jnp.bfloat16)
    act_out[...] = act
    out[...] = jnp.dot(act, w_down[:, at], preferred_element_type=jnp.float32).astype(out.dtype)


def down_kernel(core, act, w_down, out):
    half = out.shape[1]
    at = pl.ds(pl.multiple_of(core[0] * half, half), half)
    out[...] = jnp.dot(act[...], w_down[:, at], preferred_element_type=jnp.float32)


def spread_kernel(places, own, first, second, third, send):
    slots, width = own.shape
    piece = width // PARTS
    total = own[...].astype(jnp.float32) + first[...].astype(jnp.float32)
    total = total + second[...].astype(jnp.float32) + third[...].astype(jnp.float32)
    stacked = jnp.concatenate(
        [total[:, part * piece : (part + 1) * piece] for part in range(PARTS)]
        + [jnp.zeros((LANES - PARTS * slots, piece), jnp.float32)],
        axis=0,
    ).astype(jnp.bfloat16)
    send[...] = jnp.dot(places[...], stacked, preferred_element_type=jnp.float32).astype(
        jnp.bfloat16
    )


def combine_kernel(received, stream, gates, out, rows):
    peers = received.shape[0] // CORES
    piece = received.shape[2]
    half = piece * PARTS
    batches = out.shape[0]
    gate = gates[...]
    for core in range(CORES):
        total = jnp.zeros(received.shape[1:], jnp.float32)
        for peer in range(peers):
            total += received[core * peers + peer].astype(jnp.float32) * gate[:, peer : peer + 1]
        total += stream[core].astype(jnp.float32)
        for row in range(batches):
            for part in range(PARTS):
                start = core * half + part * piece
                place = row * PARTS + part
                rows[row : row + 1, start : start + piece] = total[place : place + 1]
    out[...] = rows[0:batches].astype(jnp.bfloat16)


def shards(
    residual, query, new_key, new_value, key_cache, value_cache, lengths, expert_ids,
    norm_gain, router, w_gate, w_up, w_down,
):
    batches, _, features = residual.shape
    context = key_cache.shape[2]
    kv_width = key_cache.shape[3]
    xs = lax.axis_size("x")
    peers = lax.axis_size("ep")
    half = features // CORES
    piece = half // PARTS
    slots = CORES * batches * CAP
    expert = (lax.axis_index("ep") // 2).reshape(1)
    core = lax.axis_index("core").reshape(1)
    f32, bf16 = jnp.float32, jnp.bfloat16
    hidden = w_gate.shape[2]
    params = pltpu.CompilerParams(vmem_limit_bytes=16 * 2**20)

    def in_hbm(array):
        return pltpu.with_memory_space_constraint(array, pltpu.HBM)

    def in_vmem(array):
        return pltpu.with_memory_space_constraint(array, pltpu.VMEM)

    def cost(flops, moved):
        return pl.CostEstimate(flops=flops, bytes_accessed=moved, transcendentals=0)

    with jax.named_scope("attention"):
        send, stream, gates = pl.pallas_call(
            attention_kernel,
            out_shape=(
                jax.ShapeDtypeStruct((CORES * peers, 8, piece + LANES), bf16),
                jax.ShapeDtypeStruct((CORES, 8, piece), bf16),
                jax.ShapeDtypeStruct((8, LANES), f32),
            ),
            in_specs=[SMEM, SMEM] + [ANY] * 10,
            out_specs=(VMEM, VMEM, VMEM),
            scratch_shapes=[
                pltpu.SMEM((batches,), jnp.int32),
                pltpu.SMEM((batches, 2), jnp.int32),
                pltpu.VMEM((batches, features), bf16),
                pltpu.VMEM((batches, features), bf16),
                pltpu.VMEM((batches, kv_width), bf16),
                pltpu.VMEM((batches, kv_width), bf16),
                pltpu.VMEM((1, features), f32),
                pltpu.VMEM(router.shape[::-1], bf16),
                pltpu.VMEM((batches, context, kv_width), bf16),
                pltpu.VMEM((batches, context, kv_width), bf16),
                pltpu.VMEM((batches, 8 * KV_HEADS, kv_width), f32),
                pltpu.VMEM((8, features), f32),
                pltpu.VMEM((2, 8, piece + LANES), f32),
                pltpu.SemaphoreType.DMA((2 * batches,)),
                pltpu.SemaphoreType.DMA((8,)),
            ],
            compiler_params=params,
            name="attention",
        )(
            expert,
            core,
            in_hbm(lengths.reshape(batches)),
            in_hbm(expert_ids.reshape(batches, 2)),
            in_hbm(query.reshape(batches, features)),
            in_hbm(residual.reshape(batches, features)),
            in_hbm(new_key.reshape(batches, kv_width)),
            in_hbm(new_value.reshape(batches, kv_width)),
            in_hbm(key_cache.reshape(batches, context, kv_width)),
            in_hbm(value_cache.reshape(batches, context, kv_width)),
            in_hbm(norm_gain.reshape(1, features)),
            in_hbm(router.T),
        )
    with jax.named_scope("rows_to_experts"):
        received = lax.all_to_all(send, ("core", "ep"), 0, 0, tiled=True)
    with jax.named_scope("select"):
        chosen, places = pl.pallas_call(
            select_kernel,
            out_shape=(
                jax.ShapeDtypeStruct((slots, half), bf16),
                jax.ShapeDtypeStruct((CORES * peers * 8, LANES), bf16),
            ),
            in_specs=[SMEM, VMEM],
            out_specs=(VMEM, VMEM),
            compiler_params=params,
            name="select",
        )(expert, received.reshape(CORES * peers * 8, piece + LANES))

    def along(array, step):
        return lax.ppermute(array, "x", [(i, (i + step) % xs) for i in range(xs)])

    def swap(array):
        return lax.ppermute(array, "core", [(0, 1), (1, 0)])

    with jax.named_scope("rows_along_x"):
        parts = [chosen] + [along(chosen, step) for step in range(1, xs)]
    with jax.named_scope("weights"):
        gate_here, up_here, down_here, ready = pl.pallas_call(
            fetch_kernel,
            out_shape=tuple(pltpu.VMEM(w.shape[1:], bf16) for w in (w_gate, w_up, w_down))
            + (jax.ShapeDtypeStruct((8, LANES), f32),),
            in_specs=[VMEM] + [ANY] * 3,
            out_specs=(VMEM,) * 4,
            scratch_shapes=[pltpu.SemaphoreType.DMA((12,))],
            compiler_params=pltpu.CompilerParams(vmem_limit_bytes=2**20),
            cost_estimate=cost(0, 6 * w_gate.size),
            name="weights",
        )(places, in_hbm(w_gate[0]), in_hbm(w_up[0]), in_hbm(w_down[0]))
    with jax.named_scope("join"):
        mine = pl.pallas_call(
            join_kernel,
            out_shape=jax.ShapeDtypeStruct((xs * slots, half), bf16),
            in_specs=[VMEM] * (xs + 1),
            out_specs=VMEM,
            compiler_params=params,
            name="join",
        )(ready, *parts)
    with jax.named_scope("rows_between_cores"):
        other = swap(mine)
    with jax.named_scope("near_half"):
        gate, up = pl.pallas_call(
            near_kernel,
            out_shape=(jax.ShapeDtypeStruct((mine.shape[0], hidden), f32),) * 2,
            in_specs=[SMEM, VMEM, VMEM, VMEM],
            out_specs=(VMEM, VMEM),
            compiler_params=params,
            cost_estimate=cost(2 * mine.size * 2 * hidden, 2 * w_gate.size),
            name="near_half",
        )(core, mine, in_vmem(gate_here), in_vmem(up_here))
    with jax.named_scope("far_half"):
        act, other_sum = pl.pallas_call(
            far_kernel,
            out_shape=(
                jax.ShapeDtypeStruct((mine.shape[0], hidden), bf16),
                jax.ShapeDtypeStruct(mine.shape, bf16),
            ),
            in_specs=[SMEM] + [VMEM] * 6,
            out_specs=(VMEM, VMEM),
            compiler_params=params,
            cost_estimate=cost(2 * mine.size * 3 * hidden, 3 * w_gate.size),
            name="far_half",
        )(
            core, other, gate, up,
            in_vmem(gate_here), in_vmem(up_here), in_vmem(down_here),
        )
    with jax.named_scope("sums_between_cores"):
        arrived = swap(other_sum)
    with jax.named_scope("down"):
        mine_sum = pl.pallas_call(
            down_kernel,
            out_shape=jax.ShapeDtypeStruct(mine.shape, f32),
            in_specs=[SMEM] + [VMEM] * 2,
            out_specs=VMEM,
            compiler_params=params,
            cost_estimate=cost(2 * mine.size * hidden, w_gate.size),
            name="down",
        )(core, act, in_vmem(down_here))
        total = (mine_sum + arrived.astype(f32)).astype(bf16)
    with jax.named_scope("sums_along_x"):
        total = total.reshape(xs, slots, half)
        backs = [along(total[step], xs - step) for step in range(1, xs)]
    with jax.named_scope("spread"):
        send = pl.pallas_call(
            spread_kernel,
            out_shape=jax.ShapeDtypeStruct((CORES * peers * 8, piece), bf16),
            in_specs=[VMEM] * (2 + len(backs)),
            out_specs=VMEM,
            compiler_params=params,
            name="spread",
        )(places, total[0], *backs)
    with jax.named_scope("sums_to_rows"):
        received = lax.all_to_all(
            send.reshape(CORES * peers, 8, piece), ("core", "ep"), 0, 0, tiled=True
        )
    with jax.named_scope("combine"):
        out = pl.pallas_call(
            combine_kernel,
            out_shape=jax.ShapeDtypeStruct((batches, features), bf16),
            in_specs=[VMEM, VMEM, VMEM],
            out_specs=VMEM,
            scratch_shapes=[pltpu.VMEM((8, features), f32)],
            compiler_params=params,
            name="combine",
        )(received, stream, gates)
    return out.reshape(batches, 1, features)


def solution(mesh):
    attn, ep = mesh.shape["attn"], mesh.shape["ep"]
    fine = Mesh(mesh.devices.reshape(attn // CORES, CORES, ep), ("x", "core", "ep"))
    rows = ("x", "core", "ep")
    in_specs = (
        P(None, rows, None),
        P(None, rows, None),
        P(None, rows, None),
        P(None, rows, None),
        P(None, rows, None, None),
        P(None, rows, None, None),
        P(None, rows),
        P(None, rows, None),
        P(),
        P(),
        P("ep", None, ("x", "core")),
        P("ep", None, ("x", "core")),
        P("ep", ("x", "core"), None),
    )
    return jax.shard_map(
        shards, mesh=fine, in_specs=in_specs, out_specs=P(None, rows, None), check_vma=False
    )
```

```python
import functools

import jax
import jax.numpy as jnp
from jax import lax
from jax.experimental import pallas as pl
from jax.experimental.pallas import tpu as pltpu
from jax.sharding import Mesh, PartitionSpec as P

KV_HEADS = 8
HEAD = 128
CAP = 6
CORES = 2
LANES = 128
PARTS = 8
EPSILON = 1e-05

VMEM = pl.BlockSpec(memory_space=pltpu.VMEM)
SMEM = pl.BlockSpec(memory_space=pltpu.SMEM)
ANY = pl.BlockSpec(memory_space=pl.ANY)


def iota(shape, dim):
    return lax.broadcasted_iota(jnp.int32, shape, dim)


def attention_kernel(
    expert, lengths_at, ids_at, query_at, residual_at, new_key_at, new_value_at, keys, values, gain_at,
    router_at, send, stream_out, gates_out,
    lengths, ids, query, residual, new_key, new_value, gain, router,
    key_buf, value_buf, spread, rows, packed, sems, small_sems,
):
    batches, features = query.shape
    heads = features // HEAD
    group = heads // KV_HEADS
    peers = send.shape[0]
    piece = features // PARTS
    copies = []
    for row in range(batches):
        copies.append(
            (
                pltpu.make_async_copy(keys.at[row], key_buf.at[row], sems.at[2 * row]),
                pltpu.make_async_copy(values.at[row], value_buf.at[row], sems.at[2 * row + 1]),
            )
        )
    small = [
        pltpu.make_async_copy(source, target, small_sems.at[index])
        for index, (source, target) in enumerate(
            (
                (query_at, query),
                (new_key_at, new_key),
                (new_value_at, new_value),
                (residual_at, residual),
                (gain_at, gain),
                (router_at, router),
                (lengths_at, lengths),
                (ids_at, ids),
            )
        )
    ]
    for copy in small[:3]:
        copy.start()
    for copy in copies[0]:
        copy.start()
    for copy in small[3:]:
        copy.start()
    for pair in copies[1:]:
        for copy in pair:
            copy.start()
    rows[...] = jnp.zeros_like(rows)
    spread[...] = jnp.zeros_like(spread)
    for copy in small:
        copy.wait()
    query_wide = query[...].astype(jnp.float32)
    key_wide = new_key[...].astype(jnp.float32)
    value_wide = new_value[...].astype(jnp.float32)
    for row in range(batches):
        for head in range(heads):
            block, place = head // group, head % group
            spread[row, pl.ds(8 * block + place, 1), pl.ds(HEAD * block, HEAD)] = query_wide[
                row : row + 1, HEAD * head : HEAD * (head + 1)
            ]
    for row in range(batches):
        queries = spread[row]
        own = jnp.sum(queries * key_wide[row : row + 1], axis=1, keepdims=True) * HEAD**-0.5
        copies[row][0].wait()
        scores = (
            lax.dot_general(
                queries.astype(jnp.bfloat16),
                key_buf[row],
                (((1,), (1,)), ((), ())),
                preferred_element_type=jnp.float32,
            )
            * HEAD**-0.5
        )
        scores = jnp.where(iota(scores.shape, 1) < lengths[row], scores, -jnp.inf)
        peak = jnp.maximum(jnp.max(scores, axis=1, keepdims=True), own)
        terms = jnp.exp(scores - peak)
        own_term = jnp.exp(own - peak)
        total = jnp.sum(terms, axis=1, keepdims=True) + own_term
        weights = (terms / total).astype(jnp.bfloat16)
        own_weight = (own_term / total).astype(jnp.bfloat16).astype(jnp.float32)
        copies[row][1].wait()
        mixture = jnp.dot(weights, value_buf[row], preferred_element_type=jnp.float32)
        mixture = mixture + own_weight * value_wide[row : row + 1]
        for head in range(heads):
            block, place = head // group, head % group
            rows[row : row + 1, HEAD * head : HEAD * (head + 1)] = mixture[
                8 * block + place : 8 * block + place + 1, HEAD * block : HEAD * (block + 1)
            ]
    attended = rows[0:batches].astype(jnp.bfloat16).astype(jnp.float32)
    stream = (residual[...].astype(jnp.float32) + attended).astype(jnp.bfloat16)
    stream = stream.astype(jnp.float32)
    mean_square = jnp.sum(stream * stream, axis=1, keepdims=True) * (1.0 / features)
    normed = (stream * lax.rsqrt(mean_square + EPSILON) * gain[...]).astype(jnp.bfloat16)
    normed = normed.astype(jnp.float32)
    rows[0:batches] = normed
    logits = lax.dot_general(
        rows[...].astype(jnp.bfloat16),
        router[...],
        (((1,), (1,)), ((), ())),
        preferred_element_type=jnp.float32,
    )
    for row in range(batches):
        for part in range(PARTS):
            start, place = part * piece, row * PARTS + part
            packed[0, pl.ds(place, 1), 0:piece] = normed[row : row + 1, start : start + piece]
            packed[1, pl.ds(place, 1), 0:piece] = stream[row : row + 1, start : start + piece]
        lane = iota((PARTS, LANES), 1)
        names = jnp.where(lane == 0, ids[row, 0], jnp.where(lane == 1, ids[row, 1], 0))
        packed[0, pl.ds(row * PARTS, PARTS), piece : piece + LANES] = names.astype(jnp.float32)
    chunk = packed[0].astype(jnp.bfloat16)
    for peer in range(peers):
        send[peer] = chunk
    stream_out[...] = packed[1, :, 0:piece].astype(jnp.bfloat16)
    for row in range(batches):
        lane = iota((1, logits.shape[1]), 1)
        own = logits[row : row + 1]
        first = jnp.sum(jnp.where(lane == ids[row, 0], own, 0.0), axis=1, keepdims=True)
        second = jnp.sum(jnp.where(lane == ids[row, 1], own, 0.0), axis=1, keepdims=True)
        larger = jnp.maximum(first, second)
        first, second = jnp.exp(first - larger), jnp.exp(second - larger)
        total = first + second
        expert = iota((PARTS, LANES), 1) // 2
        gates_out[pl.ds(row * PARTS, PARTS), :] = jnp.where(
            expert == ids[row, 0],
            first / total,
            jnp.where(expert == ids[row, 1], second / total, 0.0),
        )


def select_kernel(expert, received, chosen_out, places_out):
    count, width = received.shape
    piece = width - LANES
    slots = 2 * CAP
    sides = 2
    here = expert[0].astype(jnp.float32)
    names = received[:, piece:].astype(jnp.float32)
    lane = iota(names.shape, 1)
    match = jnp.where((names == here) & (lane < 2), 1.0, 0.0)
    match = jnp.sum(match, axis=1, keepdims=True)
    a, b = iota((count, count), 0), iota((count, count), 1)
    span = 2 * PARTS
    earlier = (a % span == b % span) & (b // span < a // span)
    rank = jnp.dot(
        jnp.where(earlier, 1.0, 0.0).astype(jnp.bfloat16),
        jnp.broadcast_to(match, (count, LANES)).astype(jnp.bfloat16),
        preferred_element_type=jnp.float32,
    )
    r, col = iota((count, LANES), 0), iota((count, LANES), 1)
    part, batch = r % PARTS, (r % span) // PARTS
    wide = PARTS // sides
    target = (part % wide) * (sides * slots) + (part // wide) * slots + batch * CAP
    target = target + rank.astype(jnp.int32)
    places = jnp.where((col == target) & (match > 0.5), 1.0, 0.0).astype(jnp.bfloat16)
    places_out[...] = places
    chosen = lax.dot_general(
        places,
        received[:, 0:piece],
        (((0,), (0,)), ((), ())),
        preferred_element_type=jnp.float32,
    ).astype(jnp.bfloat16).astype(jnp.float32)
    count = sides * slots
    for part in range(wide):
        chosen_out[:, part * piece : (part + 1) * piece] = chosen[
            part * count : (part + 1) * count
        ].astype(jnp.bfloat16)


def fetch_kernel(after, up_at, down_at, up, down, ready, sems):
    pieces = 4
    copies = []
    for source, target in ((up_at, up), (down_at, down)):
        rows = source.shape[0] // pieces
        for piece in range(pieces):
            at = pl.ds(piece * rows, rows)
            copies.append(
                pltpu.make_async_copy(source.at[at], target.at[at], sems.at[len(copies)])
            )
    for copy in copies:
        copy.start()
    ready[...] = jnp.zeros_like(ready)
    for copy in copies:
        copy.wait()


def join_kernel(ready, *refs):
    parts, out = refs[:-1], refs[-1]
    count = parts[0].shape[0]
    for index, part in enumerate(parts):
        out[index * count : (index + 1) * count, :] = part[...]


def whole_rows(rows, slots):
    wide = rows[...].astype(jnp.float32)
    count = wide.shape[0] // (2 * slots)
    return [
        jnp.concatenate(
            [wide[(2 * i + side) * slots : (2 * i + side + 1) * slots] for i in range(count)], axis=0
        ).astype(jnp.bfloat16)
        for side in range(2)
    ]


def half_rows(whole, slots, out):
    half = out.shape[1]
    count = whole.shape[0] // slots
    parts = []
    for i in range(count):
        for side in range(2):
            parts.append(whole[i * slots : (i + 1) * slots, side * half : (side + 1) * half])
    out[...] = jnp.concatenate(parts, axis=0).astype(out.dtype)


def expert_kernel(mine, other, w_gate, w_up, w_down, act_out, out):
    slots = 2 * CAP
    half = mine.shape[1]
    sides = [
        jnp.concatenate(pair, axis=0)
        for pair in zip(whole_rows(mine, slots), whole_rows(other, slots))
    ]
    gate, up = (
        jnp.dot(sides[0], w[0:half], preferred_element_type=jnp.float32)
        + jnp.dot(sides[1], w[half : 2 * half], preferred_element_type=jnp.float32)
        for w in (w_gate, w_up)
    )
    act = (gate * (1.0 / (1.0 + jnp.exp(-gate))) * up).astype(jnp.bfloat16)
    count = act.shape[0] // 2
    act_out[...] = act[0:count]
    half_rows(jnp.dot(act[count:], w_down[...], preferred_element_type=jnp.float32), slots, out)


def down_kernel(act, w_down, out):
    half_rows(jnp.dot(act[...], w_down[...], preferred_element_type=jnp.float32), 2 * CAP, out)


def spread_kernel(places, own, first, second, third, send):
    slots, width = own.shape
    piece = send.shape[1]
    wide = width // piece
    total = own[...].astype(jnp.float32) + first[...].astype(jnp.float32)
    total = total + second[...].astype(jnp.float32) + third[...].astype(jnp.float32)
    stacked = jnp.concatenate(
        [total[:, part * piece : (part + 1) * piece] for part in range(wide)]
        + [jnp.zeros((LANES - wide * slots, piece), jnp.float32)],
        axis=0,
    ).astype(jnp.bfloat16)
    send[...] = jnp.dot(places[...], stacked, preferred_element_type=jnp.float32).astype(
        jnp.bfloat16
    )


def combine_kernel(received, stream, gates, out, rows):
    peers, _, piece = received.shape
    batches = out.shape[0]
    gate = gates[...]
    total = stream[...].astype(jnp.float32)
    for peer in range(peers):
        total += received[peer].astype(jnp.float32) * gate[:, peer : peer + 1]
    for row in range(batches):
        for part in range(PARTS):
            place = row * PARTS + part
            rows[row : row + 1, part * piece : (part + 1) * piece] = total[place : place + 1]
    out[...] = rows[0:batches].astype(jnp.bfloat16)


def shards(
    residual, query, new_key, new_value, key_cache, value_cache, lengths, expert_ids,
    norm_gain, router, w_gate, w_up, w_down,
):
    batches, _, features = residual.shape
    context = key_cache.shape[2]
    kv_width = key_cache.shape[3]
    xs = lax.axis_size("x")
    peers = lax.axis_size("ep")
    half = features // CORES
    piece = features // PARTS
    pack = batches * PARTS
    slots = 2 * batches * CAP
    expert = (lax.axis_index("ep") // 2).reshape(1)
    f32, bf16 = jnp.float32, jnp.bfloat16
    hidden = w_gate.shape[2]
    params = pltpu.CompilerParams(vmem_limit_bytes=16 * 2**20)

    def in_hbm(array):
        return pltpu.with_memory_space_constraint(array, pltpu.HBM)

    def in_vmem(array):
        return pltpu.with_memory_space_constraint(array, pltpu.VMEM)

    def cost(flops, moved):
        return pl.CostEstimate(flops=flops, bytes_accessed=moved, transcendentals=0)

    with jax.named_scope("attention"):
        send, stream, gates = pl.pallas_call(
            attention_kernel,
            out_shape=(
                jax.ShapeDtypeStruct((peers, pack, piece + LANES), bf16),
                jax.ShapeDtypeStruct((pack, piece), bf16),
                jax.ShapeDtypeStruct((pack, LANES), f32),
            ),
            in_specs=[SMEM] + [ANY] * 10,
            out_specs=(VMEM, VMEM, VMEM),
            scratch_shapes=[
                pltpu.SMEM((batches,), jnp.int32),
                pltpu.SMEM((batches, 2), jnp.int32),
                pltpu.VMEM((batches, features), bf16),
                pltpu.VMEM((batches, features), bf16),
                pltpu.VMEM((batches, kv_width), bf16),
                pltpu.VMEM((batches, kv_width), bf16),
                pltpu.VMEM((1, features), f32),
                pltpu.VMEM(router.shape[::-1], bf16),
                pltpu.VMEM((batches, context, kv_width), bf16),
                pltpu.VMEM((batches, context, kv_width), bf16),
                pltpu.VMEM((batches, 8 * KV_HEADS, kv_width), f32),
                pltpu.VMEM((8, features), f32),
                pltpu.VMEM((2, pack, piece + LANES), f32),
                pltpu.SemaphoreType.DMA((2 * batches,)),
                pltpu.SemaphoreType.DMA((8,)),
            ],
            compiler_params=params,
            name="attention",
        )(
            expert,
            in_hbm(lengths.reshape(batches)),
            in_hbm(expert_ids.reshape(batches, 2)),
            in_hbm(query.reshape(batches, features)),
            in_hbm(residual.reshape(batches, features)),
            in_hbm(new_key.reshape(batches, kv_width)),
            in_hbm(new_value.reshape(batches, kv_width)),
            in_hbm(key_cache.reshape(batches, context, kv_width)),
            in_hbm(value_cache.reshape(batches, context, kv_width)),
            in_hbm(norm_gain.reshape(1, features)),
            in_hbm(router.T),
        )
    with jax.named_scope("rows_to_experts"):
        received = lax.all_to_all(send, "ep", 0, 0, tiled=True)
    with jax.named_scope("select"):
        chosen, places = pl.pallas_call(
            select_kernel,
            out_shape=(
                jax.ShapeDtypeStruct((slots, half), bf16),
                jax.ShapeDtypeStruct((peers * pack, LANES), bf16),
            ),
            in_specs=[SMEM, VMEM],
            out_specs=(VMEM, VMEM),
            compiler_params=params,
            name="select",
        )(expert, received.reshape(peers * pack, piece + LANES))

    def along(array, step):
        return lax.ppermute(array, "x", [(i, (i + step) % xs) for i in range(xs)])

    def swap(array):
        return lax.ppermute(array, "core", [(0, 1), (1, 0)])

    with jax.named_scope("rows_along_x"):
        steps = (1, xs - 1) + tuple(range(2, xs - 1))
        parts = [chosen] + [along(chosen, step) for step in steps]
    with jax.named_scope("weights"):
        up_here, down_here, ready = pl.pallas_call(
            fetch_kernel,
            out_shape=tuple(pltpu.VMEM(w.shape[1:], bf16) for w in (w_up, w_down))
            + (jax.ShapeDtypeStruct((8, LANES), f32),),
            in_specs=[VMEM] + [ANY] * 2,
            out_specs=(VMEM,) * 3,
            scratch_shapes=[pltpu.SemaphoreType.DMA((8,))],
            compiler_params=pltpu.CompilerParams(vmem_limit_bytes=2**20),
            cost_estimate=cost(0, 4 * w_gate.size),
            name="weights",
        )(places, in_hbm(w_up[0]), in_hbm(w_down[0]))
    with jax.named_scope("join"):
        mine = pl.pallas_call(
            join_kernel,
            out_shape=jax.ShapeDtypeStruct((xs * slots, half), bf16),
            in_specs=[VMEM] * (xs + 1),
            out_specs=VMEM,
            compiler_params=params,
            name="join",
        )(ready, *parts)
    with jax.named_scope("rows_between_cores"):
        other = swap(mine)
    weights_in = [in_vmem(w_gate[0]), in_vmem(up_here)]
    rows_here = mine.shape[0] // 2
    with jax.named_scope("experts"):
        act, other_sum = pl.pallas_call(
            expert_kernel,
            out_shape=(
                jax.ShapeDtypeStruct((rows_here, hidden), bf16),
                jax.ShapeDtypeStruct(mine.shape, bf16),
            ),
            in_specs=[VMEM] * 5,
            out_specs=(VMEM, VMEM),
            compiler_params=params,
            cost_estimate=cost(10 * mine.size * hidden, 6 * w_gate.size),
            name="experts",
        )(mine, other, *weights_in, in_vmem(down_here))
    with jax.named_scope("sums_between_cores"):
        arrived = swap(other_sum)
    with jax.named_scope("own_down"):
        mine_sum = pl.pallas_call(
            down_kernel,
            out_shape=jax.ShapeDtypeStruct(mine.shape, f32),
            in_specs=[VMEM] * 2,
            out_specs=VMEM,
            compiler_params=params,
            cost_estimate=cost(2 * mine.size * hidden, 2 * w_gate.size),
            name="own_down",
        )(act, in_vmem(down_here))
        total = (mine_sum + arrived.astype(f32)).astype(bf16)
    with jax.named_scope("sums_along_x"):
        total = total.reshape(xs, slots, half)
        backs = [along(total[1 + place], xs - step) for place, step in enumerate(steps)]
        backs = [backs[1], backs[0]] + backs[2:]
    with jax.named_scope("spread"):
        send = pl.pallas_call(
            spread_kernel,
            out_shape=jax.ShapeDtypeStruct((peers * pack, piece), bf16),
            in_specs=[VMEM] * (2 + len(backs)),
            out_specs=VMEM,
            compiler_params=params,
            name="spread",
        )(places, total[0], *backs)
    with jax.named_scope("sums_to_rows"):
        received = lax.all_to_all(
            send.reshape(peers, pack, piece), "ep", 0, 0, tiled=True
        )
    with jax.named_scope("combine"):
        out = pl.pallas_call(
            combine_kernel,
            out_shape=jax.ShapeDtypeStruct((batches, features), bf16),
            in_specs=[VMEM, VMEM, VMEM],
            out_specs=VMEM,
            scratch_shapes=[pltpu.VMEM((8, features), f32)],
            compiler_params=params,
            name="combine",
        )(received, stream, gates)
    return out.reshape(batches, 1, features)


def solution(mesh):
    attn, ep = mesh.shape["attn"], mesh.shape["ep"]
    fine = Mesh(mesh.devices.reshape(attn // CORES, CORES, ep), ("x", "core", "ep"))
    rows = ("x", "core", "ep")
    in_specs = (
        P(None, rows, None),
        P(None, rows, None),
        P(None, rows, None),
        P(None, rows, None),
        P(None, rows, None, None),
        P(None, rows, None, None),
        P(None, rows),
        P(None, rows, None),
        P(),
        P(),
        P("ep", None, ("x", "core")),
        P("ep", None, ("x", "core")),
        P("ep", ("x", "core"), None),
    )
    return jax.shard_map(
        shards, mesh=fine, in_specs=in_specs, out_specs=P(None, rows, None), check_vma=False
    )
```

```python
import functools

import jax
import jax.numpy as jnp
from jax import lax
from jax.experimental import pallas as pl
from jax.experimental.pallas import tpu as pltpu
from jax.sharding import Mesh, PartitionSpec as P

KV_HEADS = 8
HEAD = 128
CAP = 6
CORES = 2
LANES = 128
PARTS = 4
EPSILON = 1e-05

VMEM = pl.BlockSpec(memory_space=pltpu.VMEM)
SMEM = pl.BlockSpec(memory_space=pltpu.SMEM)
ANY = pl.BlockSpec(memory_space=pl.ANY)


def iota(shape, dim):
    return lax.broadcasted_iota(jnp.int32, shape, dim)


def attention_kernel(
    expert, lengths_at, ids_at, query_at, residual_at, new_key_at, new_value_at, keys, values, gain_at,
    router_at, send, stream_out, gates_out,
    lengths, ids, query, residual, new_key, new_value, gain, router,
    key_buf, value_buf, spread, mixed, base, scale, chunk, sems, small_sems,
):
    batches, features = query.shape
    heads = features // HEAD
    group = heads // KV_HEADS
    peers = send.shape[0]
    piece = features // PARTS
    copies = []
    for row in range(batches):
        copies.append(
            (
                pltpu.make_async_copy(keys.at[row], key_buf.at[row], sems.at[2 * row]),
                pltpu.make_async_copy(values.at[row], value_buf.at[row], sems.at[2 * row + 1]),
            )
        )
    small = [
        pltpu.make_async_copy(source, target, small_sems.at[index])
        for index, (source, target) in enumerate(
            (
                (query_at, query),
                (new_key_at, new_key),
                (new_value_at, new_value),
                (residual_at, residual),
                (gain_at, gain),
                (router_at, router),
                (lengths_at, lengths),
                (ids_at, ids),
            )
        )
    ]
    for copy in [small[0]] + [pair[0] for pair in copies] + small[1:]:
        copy.start()
    for pair in copies:
        pair[1].start()
    spread[...] = jnp.zeros_like(spread)
    small[0].wait()
    query_wide = query[...].astype(jnp.float32)
    for row in range(batches):
        for head in range(heads):
            block, place = head // group, head % group
            spread[row, pl.ds(8 * block + place, 1), pl.ds(HEAD * block, HEAD)] = query_wide[
                row : row + 1, HEAD * head : HEAD * (head + 1)
            ]
    scores = []
    for row in range(batches):
        copies[row][0].wait()
        scores.append(
            lax.dot_general(
                spread[row].astype(jnp.bfloat16),
                key_buf[row],
                (((1,), (1,)), ((), ())),
                preferred_element_type=jnp.float32,
            )
        )
    for copy in small[1:]:
        copy.wait()
    key_wide = new_key[...].astype(jnp.float32)
    value_wide = new_value[...].astype(jnp.float32)
    residual_wide = residual[...].astype(jnp.float32)
    router_wide = router[...].astype(jnp.float32)
    for row in range(batches):
        for part in range(PARTS):
            start, place = part * piece, row * PARTS + part
            at = pl.ds(place, 1)
            base[at, :] = residual_wide[row : row + 1, start : start + piece]
            scale[at, :] = gain[:, start : start + piece]
        lane = iota((PARTS, LANES), 1)
        names = jnp.where(lane == 0, ids[row, 0], jnp.where(lane == 1, ids[row, 1], 0))
        chunk[pl.ds(row * PARTS, PARTS), piece : piece + LANES] = names.astype(jnp.float32)
    shares = []
    for row in range(batches):
        own = jnp.sum(spread[row] * key_wide[row : row + 1], axis=1, keepdims=True) * HEAD**-0.5
        score = scores[row] * HEAD**-0.5
        score = jnp.where(iota(score.shape, 1) < lengths[row], score, -jnp.inf)
        peak = jnp.maximum(jnp.max(score, axis=1, keepdims=True), own)
        terms = jnp.exp(score - peak)
        own_term = jnp.exp(own - peak)
        total = jnp.sum(terms, axis=1, keepdims=True) + own_term
        weights = (terms / total).astype(jnp.bfloat16)
        own_weight = (own_term / total).astype(jnp.bfloat16).astype(jnp.float32)
        shares.append((weights, own_weight))
    for row in range(batches):
        weights, own_weight = shares[row]
        copies[row][1].wait()
        mixture = jnp.dot(weights, value_buf[row], preferred_element_type=jnp.float32)
        mixture = mixture + own_weight * value_wide[row : row + 1]
        for head in range(heads):
            block, place = head // group, head % group
            part, start = HEAD * head // piece, HEAD * head % piece
            mixed[pl.ds(row * PARTS + part, 1), pl.ds(start, HEAD)] = mixture[
                8 * block + place : 8 * block + place + 1, HEAD * block : HEAD * (block + 1)
            ]
    attended = mixed[...].astype(jnp.bfloat16).astype(jnp.float32)
    stream = (base[...] + attended).astype(jnp.bfloat16)
    stream_out[...] = stream
    stream = stream.astype(jnp.float32)
    squares = jnp.sum(stream * stream, axis=1, keepdims=True)
    owner = iota(squares.shape, 0) // PARTS
    mean_square = jnp.zeros_like(squares)
    for row in range(batches):
        total = jnp.sum(jnp.where(owner == row, squares, 0.0), axis=0, keepdims=True)
        mean_square = jnp.where(owner == row, total * (1.0 / features), mean_square)
    normed = (stream * lax.rsqrt(mean_square + EPSILON) * scale[...]).astype(jnp.bfloat16)
    normed = normed.astype(jnp.float32)
    chunk[:, 0:piece] = normed
    sent = chunk[...].astype(jnp.bfloat16)
    for peer in range(peers):
        send[peer] = sent
    for row in range(batches):
        logits = jnp.zeros((router.shape[0], 1), jnp.float32)
        for part in range(PARTS):
            place = row * PARTS + part
            logits += jnp.sum(
                router_wide[:, part * piece : (part + 1) * piece] * normed[place : place + 1],
                axis=1,
                keepdims=True,
            )
        name = iota(logits.shape, 0)
        first = jnp.sum(jnp.where(name == ids[row, 0], logits, 0.0), axis=0, keepdims=True)
        second = jnp.sum(jnp.where(name == ids[row, 1], logits, 0.0), axis=0, keepdims=True)
        larger = jnp.maximum(first, second)
        first, second = jnp.exp(first - larger), jnp.exp(second - larger)
        total = first + second
        expert = iota((PARTS, LANES), 1) // 2
        gates_out[pl.ds(row * PARTS, PARTS), :] = jnp.where(
            expert == ids[row, 0],
            first / total,
            jnp.where(expert == ids[row, 1], second / total, 0.0),
        )


def select_kernel(expert, received, chosen_out, places_out):
    count, width = received.shape
    piece = width - LANES
    slots = 2 * CAP
    sides = 2
    here = expert[0].astype(jnp.float32)
    names = received[:, piece:].astype(jnp.float32)
    lane = iota(names.shape, 1)
    match = jnp.where((names == here) & (lane < 2), 1.0, 0.0)
    match = jnp.sum(match, axis=1, keepdims=True)
    a, b = iota((count, count), 0), iota((count, count), 1)
    span = 2 * PARTS
    earlier = (a % span == b % span) & (b // span < a // span)
    rank = jnp.dot(
        jnp.where(earlier, 1.0, 0.0).astype(jnp.bfloat16),
        jnp.broadcast_to(match, (count, LANES)).astype(jnp.bfloat16),
        preferred_element_type=jnp.float32,
    )
    r, col = iota((count, LANES), 0), iota((count, LANES), 1)
    part, batch = r % PARTS, (r % span) // PARTS
    wide = PARTS // sides
    target = (part % wide) * (sides * slots) + (part // wide) * slots + batch * CAP
    target = target + rank.astype(jnp.int32)
    places = jnp.where((col == target) & (match > 0.5), 1.0, 0.0).astype(jnp.bfloat16)
    places_out[...] = places
    chosen = lax.dot_general(
        places,
        received[:, 0:piece],
        (((0,), (0,)), ((), ())),
        preferred_element_type=jnp.float32,
    ).astype(jnp.bfloat16).astype(jnp.float32)
    count = sides * slots
    for part in range(wide):
        chosen_out[:, part * piece : (part + 1) * piece] = chosen[
            part * count : (part + 1) * count
        ].astype(jnp.bfloat16)


def fetch_kernel(after, up_at, down_at, up, down, ready, sems):
    pieces = 4
    copies = []
    for source, target in ((up_at, up), (down_at, down)):
        rows = source.shape[0] // pieces
        for piece in range(pieces):
            at = pl.ds(piece * rows, rows)
            copies.append(
                pltpu.make_async_copy(source.at[at], target.at[at], sems.at[len(copies)])
            )
    for copy in copies:
        copy.start()
    ready[...] = jnp.zeros_like(ready)
    for copy in copies:
        copy.wait()


def join_kernel(ready, *refs):
    parts, out = refs[:-1], refs[-1]
    count = parts[0].shape[0]
    for index, part in enumerate(parts):
        out[index * count : (index + 1) * count, :] = part[...]


def whole_rows(rows, slots):
    wide = rows[...].astype(jnp.float32)
    count = wide.shape[0] // (2 * slots)
    return [
        jnp.concatenate(
            [wide[(2 * i + side) * slots : (2 * i + side + 1) * slots] for i in range(count)], axis=0
        ).astype(jnp.bfloat16)
        for side in range(2)
    ]


def half_rows(whole, slots, out):
    half = out.shape[1]
    count = whole.shape[0] // slots
    parts = []
    for i in range(count):
        for side in range(2):
            parts.append(whole[i * slots : (i + 1) * slots, side * half : (side + 1) * half])
    out[...] = jnp.concatenate(parts, axis=0).astype(out.dtype)


def expert_kernel(mine, other, w_gate, w_up, w_down, act_out, out):
    slots = 2 * CAP
    half = mine.shape[1]
    sides = [
        jnp.concatenate(pair, axis=0)
        for pair in zip(whole_rows(mine, slots), whole_rows(other, slots))
    ]
    gate, up = (
        jnp.dot(sides[0], w[0:half], preferred_element_type=jnp.float32)
        + jnp.dot(sides[1], w[half : 2 * half], preferred_element_type=jnp.float32)
        for w in (w_gate, w_up)
    )
    act = (gate * (1.0 / (1.0 + jnp.exp(-gate))) * up).astype(jnp.bfloat16)
    count = act.shape[0] // 2
    act_out[...] = act[0:count]
    half_rows(jnp.dot(act[count:], w_down[...], preferred_element_type=jnp.float32), slots, out)


def down_kernel(act, w_down, out):
    half_rows(jnp.dot(act[...], w_down[...], preferred_element_type=jnp.float32), 2 * CAP, out)


def spread_kernel(places, own, first, second, third, send):
    slots, width = own.shape
    piece = send.shape[1]
    wide = width // piece
    total = own[...].astype(jnp.float32) + first[...].astype(jnp.float32)
    total = total + second[...].astype(jnp.float32) + third[...].astype(jnp.float32)
    stacked = jnp.concatenate(
        [total[:, part * piece : (part + 1) * piece] for part in range(wide)]
        + [jnp.zeros((LANES - wide * slots, piece), jnp.float32)],
        axis=0,
    ).astype(jnp.bfloat16)
    send[...] = jnp.dot(places[...], stacked, preferred_element_type=jnp.float32).astype(
        jnp.bfloat16
    )


def combine_kernel(received, stream, gates, out, rows):
    peers, _, piece = received.shape
    batches = out.shape[0]
    gate = gates[...]
    total = stream[...].astype(jnp.float32)
    for peer in range(peers):
        total += received[peer].astype(jnp.float32) * gate[:, peer : peer + 1]
    for row in range(batches):
        for part in range(PARTS):
            place = row * PARTS + part
            rows[row : row + 1, part * piece : (part + 1) * piece] = total[place : place + 1]
    out[...] = rows[0:batches].astype(jnp.bfloat16)


def shards(
    residual, query, new_key, new_value, key_cache, value_cache, lengths, expert_ids,
    norm_gain, router, w_gate, w_up, w_down,
):
    batches, _, features = residual.shape
    context = key_cache.shape[2]
    kv_width = key_cache.shape[3]
    xs = lax.axis_size("x")
    peers = lax.axis_size("ep")
    half = features // CORES
    piece = features // PARTS
    pack = batches * PARTS
    slots = 2 * batches * CAP
    expert = (lax.axis_index("ep") // 2).reshape(1)
    f32, bf16 = jnp.float32, jnp.bfloat16
    hidden = w_gate.shape[2]
    params = pltpu.CompilerParams(vmem_limit_bytes=16 * 2**20)

    def in_hbm(array):
        return pltpu.with_memory_space_constraint(array, pltpu.HBM)

    def in_vmem(array):
        return pltpu.with_memory_space_constraint(array, pltpu.VMEM)

    def cost(flops, moved):
        return pl.CostEstimate(flops=flops, bytes_accessed=moved, transcendentals=0)

    with jax.named_scope("attention"):
        send, stream, gates = pl.pallas_call(
            attention_kernel,
            out_shape=(
                jax.ShapeDtypeStruct((peers, pack, piece + LANES), bf16),
                jax.ShapeDtypeStruct((pack, piece), bf16),
                jax.ShapeDtypeStruct((pack, LANES), f32),
            ),
            in_specs=[SMEM] + [ANY] * 10,
            out_specs=(VMEM, VMEM, VMEM),
            scratch_shapes=[
                pltpu.SMEM((batches,), jnp.int32),
                pltpu.SMEM((batches, 2), jnp.int32),
                pltpu.VMEM((batches, features), bf16),
                pltpu.VMEM((batches, features), bf16),
                pltpu.VMEM((batches, kv_width), bf16),
                pltpu.VMEM((batches, kv_width), bf16),
                pltpu.VMEM((1, features), f32),
                pltpu.VMEM(router.shape[::-1], bf16),
                pltpu.VMEM((batches, context, kv_width), bf16),
                pltpu.VMEM((batches, context, kv_width), bf16),
                pltpu.VMEM((batches, 8 * KV_HEADS, kv_width), f32),
                pltpu.VMEM((pack, piece), f32),
                pltpu.VMEM((pack, piece), f32),
                pltpu.VMEM((pack, piece), f32),
                pltpu.VMEM((pack, piece + LANES), f32),
                pltpu.SemaphoreType.DMA((2 * batches,)),
                pltpu.SemaphoreType.DMA((8,)),
            ],
            compiler_params=params,
            name="attention",
        )(
            expert,
            in_hbm(lengths.reshape(batches)),
            in_hbm(expert_ids.reshape(batches, 2)),
            in_hbm(query.reshape(batches, features)),
            in_hbm(residual.reshape(batches, features)),
            in_hbm(new_key.reshape(batches, kv_width)),
            in_hbm(new_value.reshape(batches, kv_width)),
            in_hbm(key_cache.reshape(batches, context, kv_width)),
            in_hbm(value_cache.reshape(batches, context, kv_width)),
            in_hbm(norm_gain.reshape(1, features)),
            in_hbm(router.T),
        )
    with jax.named_scope("rows_to_experts"):
        received = lax.all_to_all(send, "ep", 0, 0, tiled=True)
    with jax.named_scope("select"):
        chosen, places = pl.pallas_call(
            select_kernel,
            out_shape=(
                jax.ShapeDtypeStruct((slots, half), bf16),
                jax.ShapeDtypeStruct((peers * pack, LANES), bf16),
            ),
            in_specs=[SMEM, VMEM],
            out_specs=(VMEM, VMEM),
            compiler_params=params,
            name="select",
        )(expert, received.reshape(peers * pack, piece + LANES))

    def along(array, step):
        return lax.ppermute(array, "x", [(i, (i + step) % xs) for i in range(xs)])

    def swap(array):
        return lax.ppermute(array, "core", [(0, 1), (1, 0)])

    with jax.named_scope("rows_along_x"):
        steps = (1, xs - 1) + tuple(range(2, xs - 1))
        parts = [chosen] + [along(chosen, step) for step in steps]
    with jax.named_scope("weights"):
        up_here, down_here, ready = pl.pallas_call(
            fetch_kernel,
            out_shape=tuple(pltpu.VMEM(w.shape[1:], bf16) for w in (w_up, w_down))
            + (jax.ShapeDtypeStruct((8, LANES), f32),),
            in_specs=[VMEM] + [ANY] * 2,
            out_specs=(VMEM,) * 3,
            scratch_shapes=[pltpu.SemaphoreType.DMA((8,))],
            compiler_params=pltpu.CompilerParams(vmem_limit_bytes=2**20),
            cost_estimate=cost(0, 4 * w_gate.size),
            name="weights",
        )(places, in_hbm(w_up[0]), in_hbm(w_down[0]))
    with jax.named_scope("join"):
        mine = pl.pallas_call(
            join_kernel,
            out_shape=jax.ShapeDtypeStruct((xs * slots, half), bf16),
            in_specs=[VMEM] * (xs + 1),
            out_specs=VMEM,
            compiler_params=params,
            name="join",
        )(ready, *parts)
    with jax.named_scope("rows_between_cores"):
        other = swap(mine)
    weights_in = [in_vmem(w_gate[0]), in_vmem(up_here)]
    rows_here = mine.shape[0] // 2
    with jax.named_scope("experts"):
        act, other_sum = pl.pallas_call(
            expert_kernel,
            out_shape=(
                jax.ShapeDtypeStruct((rows_here, hidden), bf16),
                jax.ShapeDtypeStruct(mine.shape, bf16),
            ),
            in_specs=[VMEM] * 5,
            out_specs=(VMEM, VMEM),
            compiler_params=params,
            cost_estimate=cost(10 * mine.size * hidden, 6 * w_gate.size),
            name="experts",
        )(mine, other, *weights_in, in_vmem(down_here))
    with jax.named_scope("sums_between_cores"):
        arrived = swap(other_sum)
    with jax.named_scope("own_down"):
        mine_sum = pl.pallas_call(
            down_kernel,
            out_shape=jax.ShapeDtypeStruct(mine.shape, f32),
            in_specs=[VMEM] * 2,
            out_specs=VMEM,
            compiler_params=params,
            cost_estimate=cost(2 * mine.size * hidden, 2 * w_gate.size),
            name="own_down",
        )(act, in_vmem(down_here))
        total = (mine_sum + arrived.astype(f32)).astype(bf16)
    with jax.named_scope("sums_along_x"):
        total = total.reshape(xs, slots, half)
        backs = [along(total[1 + place], xs - step) for place, step in enumerate(steps)]
        backs = [backs[1], backs[0]] + backs[2:]
    with jax.named_scope("spread"):
        send = pl.pallas_call(
            spread_kernel,
            out_shape=jax.ShapeDtypeStruct((peers * pack, piece), bf16),
            in_specs=[VMEM] * (2 + len(backs)),
            out_specs=VMEM,
            compiler_params=params,
            name="spread",
        )(places, total[0], *backs)
    with jax.named_scope("sums_to_rows"):
        received = lax.all_to_all(
            send.reshape(peers, pack, piece), "ep", 0, 0, tiled=True
        )
    with jax.named_scope("combine"):
        out = pl.pallas_call(
            combine_kernel,
            out_shape=jax.ShapeDtypeStruct((batches, features), bf16),
            in_specs=[VMEM, VMEM, VMEM],
            out_specs=VMEM,
            scratch_shapes=[pltpu.VMEM((8, features), f32)],
            compiler_params=params,
            name="combine",
        )(received, stream, gates)
    return out.reshape(batches, 1, features)


def solution(mesh):
    attn, ep = mesh.shape["attn"], mesh.shape["ep"]
    fine = Mesh(mesh.devices.reshape(attn // CORES, CORES, ep), ("x", "core", "ep"))
    rows = ("x", "core", "ep")
    in_specs = (
        P(None, rows, None),
        P(None, rows, None),
        P(None, rows, None),
        P(None, rows, None),
        P(None, rows, None, None),
        P(None, rows, None, None),
        P(None, rows),
        P(None, rows, None),
        P(),
        P(),
        P("ep", None, ("x", "core")),
        P("ep", None, ("x", "core")),
        P("ep", ("x", "core"), None),
    )
    return jax.shard_map(
        shards, mesh=fine, in_specs=in_specs, out_specs=P(None, rows, None), check_vma=False
    )
```

```python
import functools

import jax
import jax.numpy as jnp
from jax import lax
from jax.experimental import pallas as pl
from jax.experimental.pallas import tpu as pltpu
from jax.sharding import Mesh, PartitionSpec as P

KV_HEADS = 8
HEAD = 128
CAP = 6
CORES = 2
LANES = 128
PARTS = 4
EPSILON = 1e-05

VMEM = pl.BlockSpec(memory_space=pltpu.VMEM)
SMEM = pl.BlockSpec(memory_space=pltpu.SMEM)
ANY = pl.BlockSpec(memory_space=pl.ANY)


def iota(shape, dim):
    return lax.broadcasted_iota(jnp.int32, shape, dim)


def attention_kernel(
    expert, lengths_at, ids_at, query_at, residual_at, new_key_at, new_value_at, keys, values, gain_at,
    send, stream_out,
    lengths, ids, query, residual, new_key, new_value, gain,
    key_buf, value_buf, spread, mixed, base, scale, chunk, sems, small_sems,
):
    batches, features = query.shape
    heads = features // HEAD
    group = heads // KV_HEADS
    peers = send.shape[0]
    piece = features // PARTS
    copies = []
    for row in range(batches):
        copies.append(
            (
                pltpu.make_async_copy(keys.at[row], key_buf.at[row], sems.at[2 * row]),
                pltpu.make_async_copy(values.at[row], value_buf.at[row], sems.at[2 * row + 1]),
            )
        )
    small = [
        pltpu.make_async_copy(source, target, small_sems.at[index])
        for index, (source, target) in enumerate(
            (
                (query_at, query),
                (new_key_at, new_key),
                (new_value_at, new_value),
                (residual_at, residual),
                (gain_at, gain),
                (lengths_at, lengths),
                (ids_at, ids),
            )
        )
    ]
    for copy in [small[0]] + [pair[0] for pair in copies] + small[1:]:
        copy.start()
    for pair in copies:
        pair[1].start()
    spread[...] = jnp.zeros_like(spread)
    small[0].wait()
    query_wide = query[...].astype(jnp.float32)
    for row in range(batches):
        for head in range(heads):
            block, place = head // group, head % group
            spread[row, pl.ds(8 * block + place, 1), pl.ds(HEAD * block, HEAD)] = query_wide[
                row : row + 1, HEAD * head : HEAD * (head + 1)
            ]
    scores = []
    for row in range(batches):
        copies[row][0].wait()
        scores.append(
            lax.dot_general(
                spread[row].astype(jnp.bfloat16),
                key_buf[row],
                (((1,), (1,)), ((), ())),
                preferred_element_type=jnp.float32,
            )
        )
    for copy in small[1:]:
        copy.wait()
    key_wide = new_key[...].astype(jnp.float32)
    value_wide = new_value[...].astype(jnp.float32)
    residual_wide = residual[...].astype(jnp.float32)
    for row in range(batches):
        for part in range(PARTS):
            start, place = part * piece, row * PARTS + part
            at = pl.ds(place, 1)
            base[at, :] = residual_wide[row : row + 1, start : start + piece]
            scale[at, :] = gain[:, start : start + piece]
        lane = iota((PARTS, LANES), 1)
        names = jnp.where(lane == 0, ids[row, 0], jnp.where(lane == 1, ids[row, 1], 0))
        chunk[pl.ds(row * PARTS, PARTS), piece : piece + LANES] = names.astype(jnp.float32)
    shares = []
    for row in range(batches):
        own = jnp.sum(spread[row] * key_wide[row : row + 1], axis=1, keepdims=True) * HEAD**-0.5
        score = scores[row] * HEAD**-0.5
        score = jnp.where(iota(score.shape, 1) < lengths[row], score, -jnp.inf)
        peak = jnp.maximum(jnp.max(score, axis=1, keepdims=True), own)
        terms = jnp.exp(score - peak)
        own_term = jnp.exp(own - peak)
        total = jnp.sum(terms, axis=1, keepdims=True) + own_term
        weights = (terms / total).astype(jnp.bfloat16)
        own_weight = (own_term / total).astype(jnp.bfloat16).astype(jnp.float32)
        shares.append((weights, own_weight))
    for row in range(batches):
        weights, own_weight = shares[row]
        copies[row][1].wait()
        mixture = jnp.dot(weights, value_buf[row], preferred_element_type=jnp.float32)
        mixture = mixture + own_weight * value_wide[row : row + 1]
        for head in range(heads):
            block, place = head // group, head % group
            part, start = HEAD * head // piece, HEAD * head % piece
            mixed[pl.ds(row * PARTS + part, 1), pl.ds(start, HEAD)] = mixture[
                8 * block + place : 8 * block + place + 1, HEAD * block : HEAD * (block + 1)
            ]
    attended = mixed[...].astype(jnp.bfloat16).astype(jnp.float32)
    stream = (base[...] + attended).astype(jnp.bfloat16)
    stream_out[...] = stream
    stream = stream.astype(jnp.float32)
    squares = jnp.sum(stream * stream, axis=1, keepdims=True)
    owner = iota(squares.shape, 0) // PARTS
    mean_square = jnp.zeros_like(squares)
    for row in range(batches):
        total = jnp.sum(jnp.where(owner == row, squares, 0.0), axis=0, keepdims=True)
        mean_square = jnp.where(owner == row, total * (1.0 / features), mean_square)
    normed = (stream * lax.rsqrt(mean_square + EPSILON) * scale[...]).astype(jnp.bfloat16)
    normed = normed.astype(jnp.float32)
    chunk[:, 0:piece] = normed
    sent = chunk[...].astype(jnp.bfloat16)
    for peer in range(peers):
        send[peer] = sent


def select_kernel(expert, received, chosen_out, places_out):
    count, width = received.shape
    piece = width - LANES
    slots = 2 * CAP
    sides = 2
    here = expert[0].astype(jnp.float32)
    names = received[:, piece:].astype(jnp.float32)
    lane = iota(names.shape, 1)
    match = jnp.where((names == here) & (lane < 2), 1.0, 0.0)
    match = jnp.sum(match, axis=1, keepdims=True)
    a, b = iota((count, count), 0), iota((count, count), 1)
    span = 2 * PARTS
    earlier = (a % span == b % span) & (b // span < a // span)
    rank = jnp.dot(
        jnp.where(earlier, 1.0, 0.0).astype(jnp.bfloat16),
        jnp.broadcast_to(match, (count, LANES)).astype(jnp.bfloat16),
        preferred_element_type=jnp.float32,
    )
    r, col = iota((count, LANES), 0), iota((count, LANES), 1)
    part, batch = r % PARTS, (r % span) // PARTS
    wide = PARTS // sides
    target = (part % wide) * (sides * slots) + (part // wide) * slots + batch * CAP
    target = target + rank.astype(jnp.int32)
    places = jnp.where((col == target) & (match > 0.5), 1.0, 0.0).astype(jnp.bfloat16)
    places_out[...] = places
    chosen = lax.dot_general(
        places,
        received[:, 0:piece],
        (((0,), (0,)), ((), ())),
        preferred_element_type=jnp.float32,
    ).astype(jnp.bfloat16).astype(jnp.float32)
    count = sides * slots
    for part in range(wide):
        chosen_out[:, part * piece : (part + 1) * piece] = chosen[
            part * count : (part + 1) * count
        ].astype(jnp.bfloat16)


def fetch_kernel(after, sent, router, up_at, down_at, up, down, gates_out, sems):
    pieces = 4
    copies = []
    for source, target in ((up_at, up), (down_at, down)):
        rows = source.shape[0] // pieces
        for piece in range(pieces):
            at = pl.ds(piece * rows, rows)
            copies.append(
                pltpu.make_async_copy(source.at[at], target.at[at], sems.at[len(copies)])
            )
    for copy in copies:
        copy.start()
    piece = sent.shape[2] - LANES
    normed = sent[0, :, 0:piece].astype(jnp.float32)
    names = sent[0, :, piece:].astype(jnp.float32)
    router_wide = router[...].astype(jnp.float32)
    for row in range(normed.shape[0] // PARTS):
        logits = jnp.zeros((router.shape[0], 1), jnp.float32)
        for part in range(PARTS):
            place = row * PARTS + part
            logits += jnp.sum(
                router_wide[:, part * piece : (part + 1) * piece] * normed[place : place + 1],
                axis=1,
                keepdims=True,
            )
        at = row * PARTS
        expert = iota(logits.shape, 0).astype(jnp.float32)
        ids = [names[at : at + 1, turn : turn + 1] for turn in range(2)]
        first, second = (
            jnp.sum(jnp.where(expert == name, logits, 0.0), axis=0, keepdims=True) for name in ids
        )
        larger = jnp.maximum(first, second)
        first, second = jnp.exp(first - larger), jnp.exp(second - larger)
        total = first + second
        holder = (iota((PARTS, LANES), 1) // 2).astype(jnp.float32)
        gates_out[pl.ds(at, PARTS), :] = jnp.where(
            holder == ids[0], first / total, jnp.where(holder == ids[1], second / total, 0.0)
        )
    for copy in copies:
        copy.wait()


def join_kernel(ready, *refs):
    parts, out = refs[:-1], refs[-1]
    count = parts[0].shape[0]
    for index, part in enumerate(parts):
        out[index * count : (index + 1) * count, :] = part[...]


def whole_rows(rows, slots):
    wide = rows[...].astype(jnp.float32)
    count = wide.shape[0] // (2 * slots)
    return [
        jnp.concatenate(
            [wide[(2 * i + side) * slots : (2 * i + side + 1) * slots] for i in range(count)], axis=0
        ).astype(jnp.bfloat16)
        for side in range(2)
    ]


def half_rows(whole, slots, out):
    half = out.shape[1]
    count = whole.shape[0] // slots
    parts = []
    for i in range(count):
        for side in range(2):
            parts.append(whole[i * slots : (i + 1) * slots, side * half : (side + 1) * half])
    out[...] = jnp.concatenate(parts, axis=0).astype(out.dtype)


def expert_kernel(mine, other, w_gate, w_up, w_down, act_out, out):
    slots = 2 * CAP
    half = mine.shape[1]
    sides = [
        jnp.concatenate(pair, axis=0)
        for pair in zip(whole_rows(mine, slots), whole_rows(other, slots))
    ]
    gate, up = (
        jnp.dot(sides[0], w[0:half], preferred_element_type=jnp.float32)
        + jnp.dot(sides[1], w[half : 2 * half], preferred_element_type=jnp.float32)
        for w in (w_gate, w_up)
    )
    act = (gate * (1.0 / (1.0 + jnp.exp(-gate))) * up).astype(jnp.bfloat16)
    count = act.shape[0] // 2
    act_out[...] = act[0:count]
    half_rows(jnp.dot(act[count:], w_down[...], preferred_element_type=jnp.float32), slots, out)


def down_kernel(act, w_down, out):
    half_rows(jnp.dot(act[...], w_down[...], preferred_element_type=jnp.float32), 2 * CAP, out)


def spread_kernel(places, own, first, second, third, send):
    slots, width = own.shape
    piece = send.shape[1]
    wide = width // piece
    total = own[...].astype(jnp.float32) + first[...].astype(jnp.float32)
    total = total + second[...].astype(jnp.float32) + third[...].astype(jnp.float32)
    stacked = jnp.concatenate(
        [total[:, part * piece : (part + 1) * piece] for part in range(wide)]
        + [jnp.zeros((LANES - wide * slots, piece), jnp.float32)],
        axis=0,
    ).astype(jnp.bfloat16)
    send[...] = jnp.dot(places[...], stacked, preferred_element_type=jnp.float32).astype(
        jnp.bfloat16
    )


def combine_kernel(received, stream, gates, out, rows):
    peers, _, piece = received.shape
    batches = out.shape[0]
    gate = gates[...]
    total = stream[...].astype(jnp.float32)
    for peer in range(peers):
        total += received[peer].astype(jnp.float32) * gate[:, peer : peer + 1]
    for row in range(batches):
        for part in range(PARTS):
            place = row * PARTS + part
            rows[row : row + 1, part * piece : (part + 1) * piece] = total[place : place + 1]
    out[...] = rows[0:batches].astype(jnp.bfloat16)


def shards(
    residual, query, new_key, new_value, key_cache, value_cache, lengths, expert_ids,
    norm_gain, router, w_gate, w_up, w_down,
):
    batches, _, features = residual.shape
    context = key_cache.shape[2]
    kv_width = key_cache.shape[3]
    xs = lax.axis_size("x")
    peers = lax.axis_size("ep")
    half = features // CORES
    piece = features // PARTS
    pack = batches * PARTS
    slots = 2 * batches * CAP
    expert = (lax.axis_index("ep") // 2).reshape(1)
    f32, bf16 = jnp.float32, jnp.bfloat16
    hidden = w_gate.shape[2]
    params = pltpu.CompilerParams(vmem_limit_bytes=16 * 2**20)

    def in_hbm(array):
        return pltpu.with_memory_space_constraint(array, pltpu.HBM)

    def in_vmem(array):
        return pltpu.with_memory_space_constraint(array, pltpu.VMEM)

    def cost(flops, moved):
        return pl.CostEstimate(flops=flops, bytes_accessed=moved, transcendentals=0)

    with jax.named_scope("attention"):
        send, stream = pl.pallas_call(
            attention_kernel,
            out_shape=(
                jax.ShapeDtypeStruct((peers, pack, piece + LANES), bf16),
                jax.ShapeDtypeStruct((pack, piece), bf16),
            ),
            in_specs=[SMEM] + [ANY] * 9,
            out_specs=(VMEM, VMEM),
            scratch_shapes=[
                pltpu.SMEM((batches,), jnp.int32),
                pltpu.SMEM((batches, 2), jnp.int32),
                pltpu.VMEM((batches, features), bf16),
                pltpu.VMEM((batches, features), bf16),
                pltpu.VMEM((batches, kv_width), bf16),
                pltpu.VMEM((batches, kv_width), bf16),
                pltpu.VMEM((1, features), f32),
                pltpu.VMEM((batches, context, kv_width), bf16),
                pltpu.VMEM((batches, context, kv_width), bf16),
                pltpu.VMEM((batches, 8 * KV_HEADS, kv_width), f32),
                pltpu.VMEM((pack, piece), f32),
                pltpu.VMEM((pack, piece), f32),
                pltpu.VMEM((pack, piece), f32),
                pltpu.VMEM((pack, piece + LANES), f32),
                pltpu.SemaphoreType.DMA((2 * batches,)),
                pltpu.SemaphoreType.DMA((8,)),
            ],
            compiler_params=params,
            name="attention",
        )(
            expert,
            in_hbm(lengths.reshape(batches)),
            in_hbm(expert_ids.reshape(batches, 2)),
            in_hbm(query.reshape(batches, features)),
            in_hbm(residual.reshape(batches, features)),
            in_hbm(new_key.reshape(batches, kv_width)),
            in_hbm(new_value.reshape(batches, kv_width)),
            in_hbm(key_cache.reshape(batches, context, kv_width)),
            in_hbm(value_cache.reshape(batches, context, kv_width)),
            in_hbm(norm_gain.reshape(1, features)),
        )
    with jax.named_scope("rows_to_experts"):
        received = lax.all_to_all(send, "ep", 0, 0, tiled=True)
    with jax.named_scope("select"):
        chosen, places = pl.pallas_call(
            select_kernel,
            out_shape=(
                jax.ShapeDtypeStruct((slots, half), bf16),
                jax.ShapeDtypeStruct((peers * pack, LANES), bf16),
            ),
            in_specs=[SMEM, VMEM],
            out_specs=(VMEM, VMEM),
            compiler_params=params,
            name="select",
        )(expert, received.reshape(peers * pack, piece + LANES))

    def along(array, step):
        return lax.ppermute(array, "x", [(i, (i + step) % xs) for i in range(xs)])

    def swap(array):
        return lax.ppermute(array, "core", [(0, 1), (1, 0)])

    with jax.named_scope("rows_along_x"):
        steps = tuple(range(2, xs - 1)) + (xs - 1, 1)
        parts = [chosen] + [along(chosen, step) for step in steps]
    with jax.named_scope("weights"):
        up_here, down_here, gates = pl.pallas_call(
            fetch_kernel,
            out_shape=tuple(pltpu.VMEM(w.shape[1:], bf16) for w in (w_up, w_down))
            + (jax.ShapeDtypeStruct((pack, LANES), f32),),
            in_specs=[VMEM] * 3 + [ANY] * 2,
            out_specs=(VMEM,) * 3,
            scratch_shapes=[pltpu.SemaphoreType.DMA((8,))],
            compiler_params=pltpu.CompilerParams(vmem_limit_bytes=2**20),
            cost_estimate=cost(0, 4 * w_gate.size),
            name="weights",
        )(places, send, router.T, in_hbm(w_up[0]), in_hbm(w_down[0]))
    with jax.named_scope("join"):
        mine = pl.pallas_call(
            join_kernel,
            out_shape=jax.ShapeDtypeStruct((xs * slots, half), bf16),
            in_specs=[VMEM] * (xs + 1),
            out_specs=VMEM,
            compiler_params=params,
            name="join",
        )(gates, *parts)
    with jax.named_scope("rows_between_cores"):
        other = swap(mine)
    weights_in = [in_vmem(w_gate[0]), in_vmem(up_here)]
    rows_here = mine.shape[0] // 2
    with jax.named_scope("experts"):
        act, other_sum = pl.pallas_call(
            expert_kernel,
            out_shape=(
                jax.ShapeDtypeStruct((rows_here, hidden), bf16),
                jax.ShapeDtypeStruct(mine.shape, bf16),
            ),
            in_specs=[VMEM] * 5,
            out_specs=(VMEM, VMEM),
            compiler_params=params,
            cost_estimate=cost(10 * mine.size * hidden, 6 * w_gate.size),
            name="experts",
        )(mine, other, *weights_in, in_vmem(down_here))
    with jax.named_scope("sums_between_cores"):
        arrived = swap(other_sum)
    with jax.named_scope("own_down"):
        mine_sum = pl.pallas_call(
            down_kernel,
            out_shape=jax.ShapeDtypeStruct(mine.shape, f32),
            in_specs=[VMEM] * 2,
            out_specs=VMEM,
            compiler_params=params,
            cost_estimate=cost(2 * mine.size * hidden, 2 * w_gate.size),
            name="own_down",
        )(act, in_vmem(down_here))
        total = (mine_sum + arrived.astype(f32)).astype(bf16)
    with jax.named_scope("sums_along_x"):
        total = total.reshape(xs, slots, half)
        backs = [along(total[1 + place], xs - step) for place, step in enumerate(steps)]
        backs = backs[:-2] + [backs[-1], backs[-2]]
    with jax.named_scope("spread"):
        send = pl.pallas_call(
            spread_kernel,
            out_shape=jax.ShapeDtypeStruct((peers * pack, piece), bf16),
            in_specs=[VMEM] * (2 + len(backs)),
            out_specs=VMEM,
            compiler_params=params,
            name="spread",
        )(places, total[0], *backs)
    with jax.named_scope("sums_to_rows"):
        received = lax.all_to_all(
            send.reshape(peers, pack, piece), "ep", 0, 0, tiled=True
        )
    with jax.named_scope("combine"):
        out = pl.pallas_call(
            combine_kernel,
            out_shape=jax.ShapeDtypeStruct((batches, features), bf16),
            in_specs=[VMEM, VMEM, VMEM],
            out_specs=VMEM,
            scratch_shapes=[pltpu.VMEM((8, features), f32)],
            compiler_params=params,
            name="combine",
        )(received, stream, gates)
    return out.reshape(batches, 1, features)


def solution(mesh):
    attn, ep = mesh.shape["attn"], mesh.shape["ep"]
    fine = Mesh(mesh.devices.reshape(attn // CORES, CORES, ep), ("x", "core", "ep"))
    rows = ("x", "core", "ep")
    in_specs = (
        P(None, rows, None),
        P(None, rows, None),
        P(None, rows, None),
        P(None, rows, None),
        P(None, rows, None, None),
        P(None, rows, None, None),
        P(None, rows),
        P(None, rows, None),
        P(),
        P(),
        P("ep", None, ("x", "core")),
        P("ep", None, ("x", "core")),
        P("ep", ("x", "core"), None),
    )
    return jax.shard_map(
        shards, mesh=fine, in_specs=in_specs, out_specs=P(None, rows, None), check_vma=False
    )
```

```python
import functools

import jax
import jax.numpy as jnp
from jax import lax
from jax.experimental import pallas as pl
from jax.experimental.pallas import tpu as pltpu
from jax.sharding import Mesh, PartitionSpec as P

KV_HEADS = 8
HEAD = 128
CAP = 6
CORES = 2
LANES = 128
PARTS = 4
EPSILON = 1e-05

VMEM = pl.BlockSpec(memory_space=pltpu.VMEM)
SMEM = pl.BlockSpec(memory_space=pltpu.SMEM)
ANY = pl.BlockSpec(memory_space=pl.ANY)


def iota(shape, dim):
    return lax.broadcasted_iota(jnp.int32, shape, dim)


def attention_kernel(
    expert, lengths_at, ids_at, query_at, residual_at, new_key_at, new_value_at, keys, values, gain_at,
    send, stream_out,
    lengths, ids, query, residual, new_key, new_value, gain,
    key_buf, value_buf, spread, mixed, base, scale, chunk, sems, small_sems,
):
    batches, features = query.shape
    heads = features // HEAD
    group = heads // KV_HEADS
    peers = send.shape[0]
    piece = features // PARTS
    copies = []
    for row in range(batches):
        copies.append(
            (
                pltpu.make_async_copy(keys.at[row], key_buf.at[row], sems.at[2 * row]),
                pltpu.make_async_copy(values.at[row], value_buf.at[row], sems.at[2 * row + 1]),
            )
        )
    small = [
        pltpu.make_async_copy(source, target, small_sems.at[index])
        for index, (source, target) in enumerate(
            (
                (query_at, query),
                (new_key_at, new_key),
                (new_value_at, new_value),
                (residual_at, residual),
                (gain_at, gain),
                (lengths_at, lengths),
                (ids_at, ids),
            )
        )
    ]
    for copy in [small[0]] + [pair[0] for pair in copies] + small[1:]:
        copy.start()
    for pair in copies:
        pair[1].start()
    spread[...] = jnp.zeros_like(spread)
    small[0].wait()
    query_wide = query[...].astype(jnp.float32)
    for row in range(batches):
        for head in range(heads):
            block, place = head // group, head % group
            spread[row, pl.ds(8 * block + place, 1), pl.ds(HEAD * block, HEAD)] = query_wide[
                row : row + 1, HEAD * head : HEAD * (head + 1)
            ]
    scores = []
    for row in range(batches):
        copies[row][0].wait()
        scores.append(
            jnp.concatenate(
                [
                    lax.dot_general(
                        spread[row, 8 * block : 8 * block + 8, lanes].astype(jnp.bfloat16),
                        key_buf[row, :, lanes],
                        (((1,), (1,)), ((), ())),
                        preferred_element_type=jnp.float32,
                    )
                    for block in range(KV_HEADS)
                    for lanes in (slice(HEAD * block, HEAD * (block + 1)),)
                ],
                axis=0,
            )
        )
    for copy in small[1:]:
        copy.wait()
    key_wide = new_key[...].astype(jnp.float32)
    value_wide = new_value[...].astype(jnp.float32)
    residual_wide = residual[...].astype(jnp.float32)
    for row in range(batches):
        for part in range(PARTS):
            start, place = part * piece, row * PARTS + part
            at = pl.ds(place, 1)
            base[at, :] = residual_wide[row : row + 1, start : start + piece]
            scale[at, :] = gain[:, start : start + piece]
        lane = iota((PARTS, LANES), 1)
        names = jnp.where(lane == 0, ids[row, 0], jnp.where(lane == 1, ids[row, 1], 0))
        chunk[pl.ds(row * PARTS, PARTS), piece : piece + LANES] = names.astype(jnp.float32)
    shares = []
    for row in range(batches):
        own = jnp.sum(spread[row] * key_wide[row : row + 1], axis=1, keepdims=True) * HEAD**-0.5
        score = scores[row] * HEAD**-0.5
        score = jnp.where(iota(score.shape, 1) < lengths[row], score, -jnp.inf)
        peak = jnp.maximum(jnp.max(score, axis=1, keepdims=True), own)
        terms = jnp.exp(score - peak)
        own_term = jnp.exp(own - peak)
        total = jnp.sum(terms, axis=1, keepdims=True) + own_term
        weights = (terms / total).astype(jnp.bfloat16).astype(jnp.float32)
        own_weight = (own_term / total).astype(jnp.bfloat16).astype(jnp.float32)
        shares.append((weights, own_weight))
    for row in range(batches):
        weights, own_weight = shares[row]
        copies[row][1].wait()
        for block in range(KV_HEADS):
            at, lanes = slice(8 * block, 8 * block + 8), slice(HEAD * block, HEAD * (block + 1))
            mixture = jnp.dot(
                weights[at].astype(jnp.bfloat16),
                value_buf[row, :, lanes],
                preferred_element_type=jnp.float32,
            )
            mixture = mixture + own_weight[at] * value_wide[row : row + 1, lanes]
            for place in range(group):
                head = block * group + place
                part, start = HEAD * head // piece, HEAD * head % piece
                mixed[pl.ds(row * PARTS + part, 1), pl.ds(start, HEAD)] = mixture[place : place + 1]
    attended = mixed[...].astype(jnp.bfloat16).astype(jnp.float32)
    stream = (base[...] + attended).astype(jnp.bfloat16)
    stream_out[...] = stream
    stream = stream.astype(jnp.float32)
    squares = jnp.sum(stream * stream, axis=1, keepdims=True)
    owner = iota(squares.shape, 0) // PARTS
    mean_square = jnp.zeros_like(squares)
    for row in range(batches):
        total = jnp.sum(jnp.where(owner == row, squares, 0.0), axis=0, keepdims=True)
        mean_square = jnp.where(owner == row, total * (1.0 / features), mean_square)
    normed = (stream * lax.rsqrt(mean_square + EPSILON) * scale[...]).astype(jnp.bfloat16)
    normed = normed.astype(jnp.float32)
    chunk[:, 0:piece] = normed
    sent = chunk[...].astype(jnp.bfloat16)
    for peer in range(peers):
        send[peer] = sent


def select_kernel(expert, received, chosen_out, places_out):
    count, width = received.shape
    piece = width - LANES
    slots = 2 * CAP
    sides = 2
    here = expert[0].astype(jnp.float32)
    names = received[:, piece:].astype(jnp.float32)
    lane = iota(names.shape, 1)
    match = jnp.where((names == here) & (lane < 2), 1.0, 0.0)
    match = jnp.sum(match, axis=1, keepdims=True)
    a, b = iota((count, count), 0), iota((count, count), 1)
    span = 2 * PARTS
    earlier = (a % span == b % span) & (b // span < a // span)
    rank = jnp.dot(
        jnp.where(earlier, 1.0, 0.0).astype(jnp.bfloat16),
        jnp.broadcast_to(match, (count, LANES)).astype(jnp.bfloat16),
        preferred_element_type=jnp.float32,
    )
    r, col = iota((count, LANES), 0), iota((count, LANES), 1)
    part, batch = r % PARTS, (r % span) // PARTS
    wide = PARTS // sides
    target = (part % wide) * (sides * slots) + (part // wide) * slots + batch * CAP
    target = target + rank.astype(jnp.int32)
    places = jnp.where((col == target) & (match > 0.5), 1.0, 0.0).astype(jnp.bfloat16)
    places_out[...] = places
    chosen = lax.dot_general(
        places,
        received[:, 0:piece],
        (((0,), (0,)), ((), ())),
        preferred_element_type=jnp.float32,
    ).astype(jnp.bfloat16).astype(jnp.float32)
    count = sides * slots
    for part in range(wide):
        chosen_out[:, part * piece : (part + 1) * piece] = chosen[
            part * count : (part + 1) * count
        ].astype(jnp.bfloat16)


def fetch_kernel(after, sent, router, up_at, down_at, up, down, gates_out, sems):
    pieces = 4
    copies = []
    for source, target in ((up_at, up), (down_at, down)):
        rows = source.shape[0] // pieces
        for piece in range(pieces):
            at = pl.ds(piece * rows, rows)
            copies.append(
                pltpu.make_async_copy(source.at[at], target.at[at], sems.at[len(copies)])
            )
    for copy in copies:
        copy.start()
    piece = sent.shape[2] - LANES
    normed = sent[0, :, 0:piece].astype(jnp.float32)
    names = sent[0, :, piece:].astype(jnp.float32)
    router_wide = router[...].astype(jnp.float32)
    for row in range(normed.shape[0] // PARTS):
        logits = jnp.zeros((router.shape[0], 1), jnp.float32)
        for part in range(PARTS):
            place = row * PARTS + part
            logits += jnp.sum(
                router_wide[:, part * piece : (part + 1) * piece] * normed[place : place + 1],
                axis=1,
                keepdims=True,
            )
        at = row * PARTS
        expert = iota(logits.shape, 0).astype(jnp.float32)
        ids = [names[at : at + 1, turn : turn + 1] for turn in range(2)]
        first, second = (
            jnp.sum(jnp.where(expert == name, logits, 0.0), axis=0, keepdims=True) for name in ids
        )
        larger = jnp.maximum(first, second)
        first, second = jnp.exp(first - larger), jnp.exp(second - larger)
        total = first + second
        holder = (iota((PARTS, LANES), 1) // 2).astype(jnp.float32)
        gates_out[pl.ds(at, PARTS), :] = jnp.where(
            holder == ids[0], first / total, jnp.where(holder == ids[1], second / total, 0.0)
        )
    for copy in copies:
        copy.wait()


def join_kernel(ready, *refs):
    parts, out = refs[:-1], refs[-1]
    count = parts[0].shape[0]
    for index, part in enumerate(parts):
        out[index * count : (index + 1) * count, :] = part[...]


def whole_rows(rows, slots):
    wide = rows[...].astype(jnp.float32)
    count = wide.shape[0] // (2 * slots)
    return [
        jnp.concatenate(
            [wide[(2 * i + side) * slots : (2 * i + side + 1) * slots] for i in range(count)], axis=0
        ).astype(jnp.bfloat16)
        for side in range(2)
    ]


def half_rows(whole, slots, out):
    half = out.shape[1]
    count = whole.shape[0] // slots
    parts = []
    for i in range(count):
        for side in range(2):
            parts.append(whole[i * slots : (i + 1) * slots, side * half : (side + 1) * half])
    out[...] = jnp.concatenate(parts, axis=0).astype(out.dtype)


def expert_kernel(mine, other, w_gate, w_up, w_down, act_out, out):
    slots = 2 * CAP
    half = mine.shape[1]
    sides = [
        jnp.concatenate(pair, axis=0)
        for pair in zip(whole_rows(mine, slots), whole_rows(other, slots))
    ]
    gate = jnp.zeros((sides[0].shape[0], w_gate.shape[1]), jnp.float32)
    up = gate
    step = 512
    for side in range(2):
        for start in range(0, half, step):
            x = sides[side][:, start : start + step]
            at = side * half + start
            gate += jnp.dot(x, w_gate[at : at + step], preferred_element_type=jnp.float32)
            up += jnp.dot(x, w_up[at : at + step], preferred_element_type=jnp.float32)
    act = (gate * (1.0 / (1.0 + jnp.exp(-gate))) * up).astype(jnp.bfloat16)
    count = act.shape[0] // 2
    act_out[...] = act[0:count]
    half_rows(jnp.dot(act[count:], w_down[...], preferred_element_type=jnp.float32), slots, out)


def down_kernel(act, w_down, out):
    half_rows(jnp.dot(act[...], w_down[...], preferred_element_type=jnp.float32), 2 * CAP, out)


def spread_kernel(places, own, first, second, third, send):
    slots, width = own.shape
    piece = send.shape[1]
    wide = width // piece
    total = own[...].astype(jnp.float32) + first[...].astype(jnp.float32)
    total = total + second[...].astype(jnp.float32) + third[...].astype(jnp.float32)
    stacked = jnp.concatenate(
        [total[:, part * piece : (part + 1) * piece] for part in range(wide)]
        + [jnp.zeros((LANES - wide * slots, piece), jnp.float32)],
        axis=0,
    ).astype(jnp.bfloat16)
    send[...] = jnp.dot(places[...], stacked, preferred_element_type=jnp.float32).astype(
        jnp.bfloat16
    )


def combine_kernel(received, stream, gates, out, rows):
    peers, _, piece = received.shape
    batches = out.shape[0]
    gate = gates[...]
    total = stream[...].astype(jnp.float32)
    for peer in range(peers):
        total += received[peer].astype(jnp.float32) * gate[:, peer : peer + 1]
    for row in range(batches):
        for part in range(PARTS):
            place = row * PARTS + part
            rows[row : row + 1, part * piece : (part + 1) * piece] = total[place : place + 1]
    out[...] = rows[0:batches].astype(jnp.bfloat16)


def shards(
    residual, query, new_key, new_value, key_cache, value_cache, lengths, expert_ids,
    norm_gain, router, w_gate, w_up, w_down,
):
    batches, _, features = residual.shape
    context = key_cache.shape[2]
    kv_width = key_cache.shape[3]
    xs = lax.axis_size("x")
    peers = lax.axis_size("ep")
    half = features // CORES
    piece = features // PARTS
    pack = batches * PARTS
    slots = 2 * batches * CAP
    expert = (lax.axis_index("ep") // 2).reshape(1)
    f32, bf16 = jnp.float32, jnp.bfloat16
    hidden = w_gate.shape[2]
    params = pltpu.CompilerParams(vmem_limit_bytes=16 * 2**20)

    def in_hbm(array):
        return pltpu.with_memory_space_constraint(array, pltpu.HBM)

    def in_vmem(array):
        return pltpu.with_memory_space_constraint(array, pltpu.VMEM)

    def cost(flops, moved):
        return pl.CostEstimate(flops=flops, bytes_accessed=moved, transcendentals=0)

    with jax.named_scope("attention"):
        send, stream = pl.pallas_call(
            attention_kernel,
            out_shape=(
                jax.ShapeDtypeStruct((peers, pack, piece + LANES), bf16),
                jax.ShapeDtypeStruct((pack, piece), bf16),
            ),
            in_specs=[SMEM] + [ANY] * 9,
            out_specs=(VMEM, VMEM),
            scratch_shapes=[
                pltpu.SMEM((batches,), jnp.int32),
                pltpu.SMEM((batches, 2), jnp.int32),
                pltpu.VMEM((batches, features), bf16),
                pltpu.VMEM((batches, features), bf16),
                pltpu.VMEM((batches, kv_width), bf16),
                pltpu.VMEM((batches, kv_width), bf16),
                pltpu.VMEM((1, features), f32),
                pltpu.VMEM((batches, context, kv_width), bf16),
                pltpu.VMEM((batches, context, kv_width), bf16),
                pltpu.VMEM((batches, 8 * KV_HEADS, kv_width), f32),
                pltpu.VMEM((pack, piece), f32),
                pltpu.VMEM((pack, piece), f32),
                pltpu.VMEM((pack, piece), f32),
                pltpu.VMEM((pack, piece + LANES), f32),
                pltpu.SemaphoreType.DMA((2 * batches,)),
                pltpu.SemaphoreType.DMA((8,)),
            ],
            compiler_params=params,
            name="attention",
        )(
            expert,
            in_hbm(lengths.reshape(batches)),
            in_hbm(expert_ids.reshape(batches, 2)),
            in_hbm(query.reshape(batches, features)),
            in_hbm(residual.reshape(batches, features)),
            in_hbm(new_key.reshape(batches, kv_width)),
            in_hbm(new_value.reshape(batches, kv_width)),
            in_hbm(key_cache.reshape(batches, context, kv_width)),
            in_hbm(value_cache.reshape(batches, context, kv_width)),
            in_hbm(norm_gain.reshape(1, features)),
        )
    with jax.named_scope("rows_to_experts"):
        received = lax.all_to_all(send, "ep", 0, 0, tiled=True)
    with jax.named_scope("select"):
        chosen, places = pl.pallas_call(
            select_kernel,
            out_shape=(
                jax.ShapeDtypeStruct((slots, half), bf16),
                jax.ShapeDtypeStruct((peers * pack, LANES), bf16),
            ),
            in_specs=[SMEM, VMEM],
            out_specs=(VMEM, VMEM),
            compiler_params=params,
            name="select",
        )(expert, received.reshape(peers * pack, piece + LANES))

    def along(array, step):
        return lax.ppermute(array, "x", [(i, (i + step) % xs) for i in range(xs)])

    def swap(array):
        return lax.ppermute(array, "core", [(0, 1), (1, 0)])

    with jax.named_scope("rows_along_x"):
        steps = tuple(range(2, xs - 1)) + (xs - 1, 1)
        parts = [chosen] + [along(chosen, step) for step in steps]
    with jax.named_scope("weights"):
        up_here, down_here, gates = pl.pallas_call(
            fetch_kernel,
            out_shape=tuple(pltpu.VMEM(w.shape[1:], bf16) for w in (w_up, w_down))
            + (jax.ShapeDtypeStruct((pack, LANES), f32),),
            in_specs=[VMEM] * 3 + [ANY] * 2,
            out_specs=(VMEM,) * 3,
            scratch_shapes=[pltpu.SemaphoreType.DMA((8,))],
            compiler_params=pltpu.CompilerParams(vmem_limit_bytes=2**20),
            cost_estimate=cost(0, 4 * w_gate.size),
            name="weights",
        )(places, send, router.T, in_hbm(w_up[0]), in_hbm(w_down[0]))
    with jax.named_scope("join"):
        mine = pl.pallas_call(
            join_kernel,
            out_shape=jax.ShapeDtypeStruct((xs * slots, half), bf16),
            in_specs=[VMEM] * (xs + 1),
            out_specs=VMEM,
            compiler_params=params,
            name="join",
        )(gates, *parts)
    with jax.named_scope("rows_between_cores"):
        other = swap(mine)
    weights_in = [in_vmem(w_gate[0]), in_vmem(up_here)]
    rows_here = mine.shape[0] // 2
    with jax.named_scope("experts"):
        act, other_sum = pl.pallas_call(
            expert_kernel,
            out_shape=(
                jax.ShapeDtypeStruct((rows_here, hidden), bf16),
                jax.ShapeDtypeStruct(mine.shape, bf16),
            ),
            in_specs=[VMEM] * 5,
            out_specs=(VMEM, VMEM),
            compiler_params=params,
            cost_estimate=cost(10 * mine.size * hidden, 6 * w_gate.size),
            name="experts",
        )(mine, other, *weights_in, in_vmem(down_here))
    with jax.named_scope("sums_between_cores"):
        arrived = swap(other_sum)
    with jax.named_scope("own_down"):
        mine_sum = pl.pallas_call(
            down_kernel,
            out_shape=jax.ShapeDtypeStruct(mine.shape, f32),
            in_specs=[VMEM] * 2,
            out_specs=VMEM,
            compiler_params=params,
            cost_estimate=cost(2 * mine.size * hidden, 2 * w_gate.size),
            name="own_down",
        )(act, in_vmem(down_here))
        total = (mine_sum + arrived.astype(f32)).astype(bf16)
    with jax.named_scope("sums_along_x"):
        total = total.reshape(xs, slots, half)
        backs = [along(total[1 + place], xs - step) for place, step in enumerate(steps)]
        backs = backs[:-2] + [backs[-1], backs[-2]]
    with jax.named_scope("spread"):
        send = pl.pallas_call(
            spread_kernel,
            out_shape=jax.ShapeDtypeStruct((peers * pack, piece), bf16),
            in_specs=[VMEM] * (2 + len(backs)),
            out_specs=VMEM,
            compiler_params=params,
            name="spread",
        )(places, total[0], *backs)
    with jax.named_scope("sums_to_rows"):
        received = lax.all_to_all(
            send.reshape(peers, pack, piece), "ep", 0, 0, tiled=True
        )
    with jax.named_scope("combine"):
        out = pl.pallas_call(
            combine_kernel,
            out_shape=jax.ShapeDtypeStruct((batches, features), bf16),
            in_specs=[VMEM, VMEM, VMEM],
            out_specs=VMEM,
            scratch_shapes=[pltpu.VMEM((8, features), f32)],
            compiler_params=params,
            name="combine",
        )(received, stream, gates)
    return out.reshape(batches, 1, features)


def solution(mesh):
    attn, ep = mesh.shape["attn"], mesh.shape["ep"]
    fine = Mesh(mesh.devices.reshape(attn // CORES, CORES, ep), ("x", "core", "ep"))
    rows = ("x", "core", "ep")
    in_specs = (
        P(None, rows, None),
        P(None, rows, None),
        P(None, rows, None),
        P(None, rows, None),
        P(None, rows, None, None),
        P(None, rows, None, None),
        P(None, rows),
        P(None, rows, None),
        P(),
        P(),
        P("ep", None, ("x", "core")),
        P("ep", None, ("x", "core")),
        P("ep", ("x", "core"), None),
    )
    return jax.shard_map(
        shards, mesh=fine, in_specs=in_specs, out_specs=P(None, rows, None), check_vma=False
    )
```

```python
import functools

import jax
import jax.numpy as jnp
from jax import lax
from jax.experimental import pallas as pl
from jax.experimental.pallas import tpu as pltpu
from jax.sharding import Mesh, PartitionSpec as P

KV_HEADS = 8
HEAD = 128
CAP = 6
CORES = 2
LANES = 128
PARTS = 4
EPSILON = 1e-05

VMEM = pl.BlockSpec(memory_space=pltpu.VMEM)
SMEM = pl.BlockSpec(memory_space=pltpu.SMEM)
ANY = pl.BlockSpec(memory_space=pl.ANY)


def iota(shape, dim):
    return lax.broadcasted_iota(jnp.int32, shape, dim)


def attention_kernel(
    expert, lengths_at, ids_at, query_at, residual_at, new_key_at, new_value_at, keys, values, gain_at,
    send, stream_out,
    lengths, ids, query, residual, new_key, new_value, gain,
    key_buf, value_buf, spread, mixed, base, scale, chunk, sems, small_sems,
):
    batches, features = query.shape
    heads = features // HEAD
    group = heads // KV_HEADS
    peers = send.shape[0]
    piece = features // PARTS
    copies = []
    for row in range(batches):
        copies.append(
            (
                pltpu.make_async_copy(keys.at[row], key_buf.at[row], sems.at[2 * row]),
                pltpu.make_async_copy(values.at[row], value_buf.at[row], sems.at[2 * row + 1]),
            )
        )
    small = [
        pltpu.make_async_copy(source, target, small_sems.at[index])
        for index, (source, target) in enumerate(
            (
                (query_at, query),
                (new_key_at, new_key),
                (new_value_at, new_value),
                (residual_at, residual),
                (gain_at, gain),
                (lengths_at, lengths),
                (ids_at, ids),
            )
        )
    ]
    for copy in [small[0]] + [pair[0] for pair in copies] + [pair[1] for pair in copies]:
        copy.start()
    for copy in small[1:]:
        copy.start()
    spread[...] = jnp.zeros_like(spread)
    small[0].wait()
    query_wide = query[...].astype(jnp.float32)
    for row in range(batches):
        for head in range(heads):
            block, place = head // group, head % group
            spread[row, pl.ds(8 * block + place, 1), pl.ds(HEAD * block, HEAD)] = query_wide[
                row : row + 1, HEAD * head : HEAD * (head + 1)
            ]
    scores = []
    for row in range(batches):
        copies[row][0].wait()
        scores.append(
            jnp.concatenate(
                [
                    lax.dot_general(
                        spread[row, 8 * block : 8 * block + 8, lanes].astype(jnp.bfloat16),
                        key_buf[row, :, lanes],
                        (((1,), (1,)), ((), ())),
                        preferred_element_type=jnp.float32,
                    )
                    for block in range(KV_HEADS)
                    for lanes in (slice(HEAD * block, HEAD * (block + 1)),)
                ],
                axis=0,
            )
        )
    for copy in small[1:]:
        copy.wait()
    key_wide = new_key[...].astype(jnp.float32)
    value_wide = new_value[...].astype(jnp.float32)
    residual_wide = residual[...].astype(jnp.float32)
    for row in range(batches):
        for part in range(PARTS):
            start, place = part * piece, row * PARTS + part
            at = pl.ds(place, 1)
            base[at, :] = residual_wide[row : row + 1, start : start + piece]
            scale[at, :] = gain[:, start : start + piece]
        lane = iota((PARTS, LANES), 1)
        names = jnp.where(lane == 0, ids[row, 0], jnp.where(lane == 1, ids[row, 1], 0))
        chunk[pl.ds(row * PARTS, PARTS), piece : piece + LANES] = names.astype(jnp.float32)
    shares = []
    for row in range(batches):
        own = jnp.sum(spread[row] * key_wide[row : row + 1], axis=1, keepdims=True) * HEAD**-0.5
        score = scores[row] * HEAD**-0.5
        score = jnp.where(iota(score.shape, 1) < lengths[row], score, -jnp.inf)
        peak = jnp.maximum(jnp.max(score, axis=1, keepdims=True), own)
        terms = jnp.exp(score - peak)
        own_term = jnp.exp(own - peak)
        total = jnp.sum(terms, axis=1, keepdims=True) + own_term
        weights = (terms / total).astype(jnp.bfloat16).astype(jnp.float32)
        own_weight = (own_term / total).astype(jnp.bfloat16).astype(jnp.float32)
        shares.append((weights, own_weight))
    for row in range(batches):
        weights, own_weight = shares[row]
        copies[row][1].wait()
        for block in range(KV_HEADS):
            at, lanes = slice(8 * block, 8 * block + 8), slice(HEAD * block, HEAD * (block + 1))
            mixture = jnp.dot(
                weights[at].astype(jnp.bfloat16),
                value_buf[row, :, lanes],
                preferred_element_type=jnp.float32,
            )
            mixture = mixture + own_weight[at] * value_wide[row : row + 1, lanes]
            for place in range(group):
                head = block * group + place
                part, start = HEAD * head // piece, HEAD * head % piece
                mixed[pl.ds(row * PARTS + part, 1), pl.ds(start, HEAD)] = mixture[place : place + 1]
    attended = mixed[...].astype(jnp.bfloat16).astype(jnp.float32)
    stream = (base[...] + attended).astype(jnp.bfloat16)
    stream_out[...] = stream
    stream = stream.astype(jnp.float32)
    squares = jnp.sum(stream * stream, axis=1, keepdims=True)
    owner = iota(squares.shape, 0) // PARTS
    mean_square = jnp.zeros_like(squares)
    for row in range(batches):
        total = jnp.sum(jnp.where(owner == row, squares, 0.0), axis=0, keepdims=True)
        mean_square = jnp.where(owner == row, total * (1.0 / features), mean_square)
    normed = (stream * lax.rsqrt(mean_square + EPSILON) * scale[...]).astype(jnp.bfloat16)
    normed = normed.astype(jnp.float32)
    chunk[:, 0:piece] = normed
    sent = chunk[...].astype(jnp.bfloat16)
    for peer in range(peers):
        send[peer] = sent


def select_kernel(expert, received, chosen_out, places_out):
    count, width = received.shape
    piece = width - LANES
    slots = 2 * CAP
    sides = 2
    here = expert[0].astype(jnp.float32)
    names = received[:, piece:].astype(jnp.float32)
    lane = iota(names.shape, 1)
    match = jnp.where((names == here) & (lane < 2), 1.0, 0.0)
    match = jnp.sum(match, axis=1, keepdims=True)
    a, b = iota((count, count), 0), iota((count, count), 1)
    span = 2 * PARTS
    earlier = (a % span == b % span) & (b // span < a // span)
    rank = jnp.dot(
        jnp.where(earlier, 1.0, 0.0).astype(jnp.bfloat16),
        jnp.broadcast_to(match, (count, LANES)).astype(jnp.bfloat16),
        preferred_element_type=jnp.float32,
    )
    r, col = iota((count, LANES), 0), iota((count, LANES), 1)
    part, batch = r % PARTS, (r % span) // PARTS
    wide = PARTS // sides
    target = (part % wide) * (sides * slots) + (part // wide) * slots + batch * CAP
    target = target + rank.astype(jnp.int32)
    places = jnp.where((col == target) & (match > 0.5), 1.0, 0.0).astype(jnp.bfloat16)
    places_out[...] = places
    chosen = lax.dot_general(
        places,
        received[:, 0:piece],
        (((0,), (0,)), ((), ())),
        preferred_element_type=jnp.float32,
    ).astype(jnp.bfloat16).astype(jnp.float32)
    count = sides * slots
    for part in range(wide):
        chosen_out[:, part * piece : (part + 1) * piece] = chosen[
            part * count : (part + 1) * count
        ].astype(jnp.bfloat16)


def fetch_kernel(after, sent, router, up_at, down_at, up, down, gates_out, sems):
    pieces = 4
    copies = []
    for source, target in ((up_at, up), (down_at, down)):
        rows = source.shape[0] // pieces
        for piece in range(pieces):
            at = pl.ds(piece * rows, rows)
            copies.append(
                pltpu.make_async_copy(source.at[at], target.at[at], sems.at[len(copies)])
            )
    for copy in copies:
        copy.start()
    piece = sent.shape[2] - LANES
    normed = sent[0, :, 0:piece].astype(jnp.float32)
    names = sent[0, :, piece:].astype(jnp.float32)
    router_wide = router[...].astype(jnp.float32)
    for row in range(normed.shape[0] // PARTS):
        logits = jnp.zeros((router.shape[0], 1), jnp.float32)
        for part in range(PARTS):
            place = row * PARTS + part
            logits += jnp.sum(
                router_wide[:, part * piece : (part + 1) * piece] * normed[place : place + 1],
                axis=1,
                keepdims=True,
            )
        at = row * PARTS
        expert = iota(logits.shape, 0).astype(jnp.float32)
        ids = [names[at : at + 1, turn : turn + 1] for turn in range(2)]
        first, second = (
            jnp.sum(jnp.where(expert == name, logits, 0.0), axis=0, keepdims=True) for name in ids
        )
        larger = jnp.maximum(first, second)
        first, second = jnp.exp(first - larger), jnp.exp(second - larger)
        total = first + second
        holder = (iota((PARTS, LANES), 1) // 2).astype(jnp.float32)
        gates_out[pl.ds(at, PARTS), :] = jnp.where(
            holder == ids[0], first / total, jnp.where(holder == ids[1], second / total, 0.0)
        )
    for copy in copies:
        copy.wait()


def join_kernel(ready, *refs):
    parts, out = refs[:-1], refs[-1]
    count = parts[0].shape[0]
    for index, part in enumerate(parts):
        out[index * count : (index + 1) * count, :] = part[...]


def whole_rows(rows, slots):
    wide = rows[...].astype(jnp.float32)
    count = wide.shape[0] // (2 * slots)
    return [
        jnp.concatenate(
            [wide[(2 * i + side) * slots : (2 * i + side + 1) * slots] for i in range(count)], axis=0
        ).astype(jnp.bfloat16)
        for side in range(2)
    ]


def half_rows(whole, slots, out):
    half = out.shape[1]
    count = whole.shape[0] // slots
    parts = []
    for i in range(count):
        for side in range(2):
            parts.append(whole[i * slots : (i + 1) * slots, side * half : (side + 1) * half])
    out[...] = jnp.concatenate(parts, axis=0).astype(out.dtype)


def expert_kernel(mine, other, w_gate, w_up, w_down, act_out, out):
    slots = 2 * CAP
    half = mine.shape[1]
    sides = [
        jnp.concatenate(pair, axis=0)
        for pair in zip(whole_rows(mine, slots), whole_rows(other, slots))
    ]
    gate = jnp.zeros((sides[0].shape[0], w_gate.shape[1]), jnp.float32)
    up = gate
    step = 512
    for side in range(2):
        for start in range(0, half, step):
            x = sides[side][:, start : start + step]
            at = side * half + start
            gate += jnp.dot(x, w_gate[at : at + step], preferred_element_type=jnp.float32)
            up += jnp.dot(x, w_up[at : at + step], preferred_element_type=jnp.float32)
    act = (gate * (1.0 / (1.0 + jnp.exp(-gate))) * up).astype(jnp.bfloat16)
    count = act.shape[0] // 2
    act_out[...] = act[0:count]
    half_rows(jnp.dot(act[count:], w_down[...], preferred_element_type=jnp.float32), slots, out)


def down_kernel(act, w_down, out):
    half_rows(jnp.dot(act[...], w_down[...], preferred_element_type=jnp.float32), 2 * CAP, out)


def spread_kernel(places, own, first, second, third, send):
    slots, width = own.shape
    piece = send.shape[1]
    wide = width // piece
    total = own[...].astype(jnp.float32) + first[...].astype(jnp.float32)
    total = total + second[...].astype(jnp.float32) + third[...].astype(jnp.float32)
    stacked = jnp.concatenate(
        [total[:, part * piece : (part + 1) * piece] for part in range(wide)]
        + [jnp.zeros((LANES - wide * slots, piece), jnp.float32)],
        axis=0,
    ).astype(jnp.bfloat16)
    send[...] = jnp.dot(places[...], stacked, preferred_element_type=jnp.float32).astype(
        jnp.bfloat16
    )


def combine_kernel(received, stream, gates, out, rows):
    peers, _, piece = received.shape
    batches = out.shape[0]
    gate = gates[...]
    total = stream[...].astype(jnp.float32)
    for peer in range(peers):
        total += received[peer].astype(jnp.float32) * gate[:, peer : peer + 1]
    for row in range(batches):
        for part in range(PARTS):
            place = row * PARTS + part
            rows[row : row + 1, part * piece : (part + 1) * piece] = total[place : place + 1]
    out[...] = rows[0:batches].astype(jnp.bfloat16)


def shards(
    residual, query, new_key, new_value, key_cache, value_cache, lengths, expert_ids,
    norm_gain, router, w_gate, w_up, w_down,
):
    batches, _, features = residual.shape
    context = key_cache.shape[2]
    kv_width = key_cache.shape[3]
    xs = lax.axis_size("x")
    peers = lax.axis_size("ep")
    half = features // CORES
    piece = features // PARTS
    pack = batches * PARTS
    slots = 2 * batches * CAP
    expert = (lax.axis_index("ep") // 2).reshape(1)
    f32, bf16 = jnp.float32, jnp.bfloat16
    hidden = w_gate.shape[2]
    params = pltpu.CompilerParams(vmem_limit_bytes=16 * 2**20)

    def in_hbm(array):
        return pltpu.with_memory_space_constraint(array, pltpu.HBM)

    def in_vmem(array):
        return pltpu.with_memory_space_constraint(array, pltpu.VMEM)

    def cost(flops, moved):
        return pl.CostEstimate(flops=flops, bytes_accessed=moved, transcendentals=0)

    with jax.named_scope("attention"):
        send, stream = pl.pallas_call(
            attention_kernel,
            out_shape=(
                jax.ShapeDtypeStruct((peers, pack, piece + LANES), bf16),
                jax.ShapeDtypeStruct((pack, piece), bf16),
            ),
            in_specs=[SMEM] + [ANY] * 9,
            out_specs=(VMEM, VMEM),
            scratch_shapes=[
                pltpu.SMEM((batches,), jnp.int32),
                pltpu.SMEM((batches, 2), jnp.int32),
                pltpu.VMEM((batches, features), bf16),
                pltpu.VMEM((batches, features), bf16),
                pltpu.VMEM((batches, kv_width), bf16),
                pltpu.VMEM((batches, kv_width), bf16),
                pltpu.VMEM((1, features), f32),
                pltpu.VMEM((batches, context, kv_width), bf16),
                pltpu.VMEM((batches, context, kv_width), bf16),
                pltpu.VMEM((batches, 8 * KV_HEADS, kv_width), f32),
                pltpu.VMEM((pack, piece), f32),
                pltpu.VMEM((pack, piece), f32),
                pltpu.VMEM((pack, piece), f32),
                pltpu.VMEM((pack, piece + LANES), f32),
                pltpu.SemaphoreType.DMA((2 * batches,)),
                pltpu.SemaphoreType.DMA((8,)),
            ],
            compiler_params=params,
            name="attention",
        )(
            expert,
            in_hbm(lengths.reshape(batches)),
            in_hbm(expert_ids.reshape(batches, 2)),
            in_hbm(query.reshape(batches, features)),
            in_hbm(residual.reshape(batches, features)),
            in_hbm(new_key.reshape(batches, kv_width)),
            in_hbm(new_value.reshape(batches, kv_width)),
            in_hbm(key_cache.reshape(batches, context, kv_width)),
            in_hbm(value_cache.reshape(batches, context, kv_width)),
            in_hbm(norm_gain.reshape(1, features)),
        )
    with jax.named_scope("rows_to_experts"):
        received = lax.all_to_all(send, "ep", 0, 0, tiled=True)
    with jax.named_scope("select"):
        chosen, places = pl.pallas_call(
            select_kernel,
            out_shape=(
                jax.ShapeDtypeStruct((slots, half), bf16),
                jax.ShapeDtypeStruct((peers * pack, LANES), bf16),
            ),
            in_specs=[SMEM, VMEM],
            out_specs=(VMEM, VMEM),
            compiler_params=params,
            name="select",
        )(expert, received.reshape(peers * pack, piece + LANES))

    def along(array, step):
        return lax.ppermute(array, "x", [(i, (i + step) % xs) for i in range(xs)])

    def swap(array):
        return lax.ppermute(array, "core", [(0, 1), (1, 0)])

    with jax.named_scope("rows_along_x"):
        steps = tuple(range(2, xs - 1)) + (xs - 1, 1)
        parts = [chosen] + [along(chosen, step) for step in steps]
    with jax.named_scope("weights"):
        up_here, down_here, gates = pl.pallas_call(
            fetch_kernel,
            out_shape=tuple(pltpu.VMEM(w.shape[1:], bf16) for w in (w_up, w_down))
            + (jax.ShapeDtypeStruct((pack, LANES), f32),),
            in_specs=[VMEM] * 3 + [ANY] * 2,
            out_specs=(VMEM,) * 3,
            scratch_shapes=[pltpu.SemaphoreType.DMA((8,))],
            compiler_params=pltpu.CompilerParams(vmem_limit_bytes=2**20),
            cost_estimate=cost(0, 4 * w_gate.size),
            name="weights",
        )(places, send, router.T, in_hbm(w_up[0]), in_hbm(w_down[0]))
    with jax.named_scope("join"):
        mine = pl.pallas_call(
            join_kernel,
            out_shape=jax.ShapeDtypeStruct((xs * slots, half), bf16),
            in_specs=[VMEM] * (xs + 1),
            out_specs=VMEM,
            compiler_params=params,
            name="join",
        )(gates, *parts)
    with jax.named_scope("rows_between_cores"):
        other = swap(mine)
    weights_in = [in_vmem(w_gate[0]), in_vmem(up_here)]
    rows_here = mine.shape[0] // 2
    with jax.named_scope("experts"):
        act, other_sum = pl.pallas_call(
            expert_kernel,
            out_shape=(
                jax.ShapeDtypeStruct((rows_here, hidden), bf16),
                jax.ShapeDtypeStruct(mine.shape, bf16),
            ),
            in_specs=[VMEM] * 5,
            out_specs=(VMEM, VMEM),
            compiler_params=params,
            cost_estimate=cost(10 * mine.size * hidden, 6 * w_gate.size),
            name="experts",
        )(mine, other, *weights_in, in_vmem(down_here))
    with jax.named_scope("sums_between_cores"):
        arrived = swap(other_sum)
    with jax.named_scope("own_down"):
        mine_sum = pl.pallas_call(
            down_kernel,
            out_shape=jax.ShapeDtypeStruct(mine.shape, f32),
            in_specs=[VMEM] * 2,
            out_specs=VMEM,
            compiler_params=params,
            cost_estimate=cost(2 * mine.size * hidden, 2 * w_gate.size),
            name="own_down",
        )(act, in_vmem(down_here))
        total = (mine_sum + arrived.astype(f32)).astype(bf16)
    with jax.named_scope("sums_along_x"):
        total = total.reshape(xs, slots, half)
        backs = [along(total[1 + place], xs - step) for place, step in enumerate(steps)]
        backs = backs[:-2] + [backs[-1], backs[-2]]
    with jax.named_scope("spread"):
        send = pl.pallas_call(
            spread_kernel,
            out_shape=jax.ShapeDtypeStruct((peers * pack, piece), bf16),
            in_specs=[VMEM] * (2 + len(backs)),
            out_specs=VMEM,
            compiler_params=params,
            name="spread",
        )(places, total[0], *backs)
    with jax.named_scope("sums_to_rows"):
        received = lax.all_to_all(
            send.reshape(peers, pack, piece), "ep", 0, 0, tiled=True
        )
    with jax.named_scope("combine"):
        out = pl.pallas_call(
            combine_kernel,
            out_shape=jax.ShapeDtypeStruct((batches, features), bf16),
            in_specs=[VMEM, VMEM, VMEM],
            out_specs=VMEM,
            scratch_shapes=[pltpu.VMEM((8, features), f32)],
            compiler_params=params,
            name="combine",
        )(received, stream, gates)
    return out.reshape(batches, 1, features)


def solution(mesh):
    attn, ep = mesh.shape["attn"], mesh.shape["ep"]
    fine = Mesh(mesh.devices.reshape(attn // CORES, CORES, ep), ("x", "core", "ep"))
    rows = ("x", "core", "ep")
    in_specs = (
        P(None, rows, None),
        P(None, rows, None),
        P(None, rows, None),
        P(None, rows, None),
        P(None, rows, None, None),
        P(None, rows, None, None),
        P(None, rows),
        P(None, rows, None),
        P(),
        P(),
        P("ep", None, ("x", "core")),
        P("ep", None, ("x", "core")),
        P("ep", ("x", "core"), None),
    )
    return jax.shard_map(
        shards, mesh=fine, in_specs=in_specs, out_specs=P(None, rows, None), check_vma=False
    )
```
